32 devices in a mesh: seq: 8 (over y, x, core), section: 4 (over z).
Axes of the slice: x: 2, y: 2, z: 4, core: 2. Of those that a mesh axis runs over, the one named last changes fastest.
Arguments:
- queries: bfloat16 [1024, 2048], P('seq', 'section'), may hold values from -10 to 10
- keys: bfloat16 [1024, 512], P('seq', 'section'), may hold values from -10 to 10
- values: bfloat16 [1024, 512], P('seq', 'section'), may hold values from -18 to 18
- residual: bfloat16 [1024, 8192], P(None, 'seq'), may hold values from -8 to 8
- out_weight: bfloat16 [2048, 8192], P('section', 'seq'), may hold values from -0.125 to 0.125
- norm_gain: float32 [8192], P('seq'), may hold values from 0.1 to 1.9
- in_weight: bfloat16 [8192, 2, 8, 256], P('seq', None, None, 'section'), may hold values from -0.09375 to 0.09375
- conv_weight: float32 [2048, 4], P(('seq', 'section')), may hold values from -3 to 3
- conv_bias: float32 [2048], P(('seq', 'section')), may hold values from -0.5 to 0.5
- proj_weight: bfloat16 [2048, 272], P(('seq', 'section')), may hold values from -0.125 to 0.125
- dt_weight: bfloat16 [256, 2048], P(None, ('seq', 'section')), may hold values from -0.375 to 0.375
- dt_bias: float32 [2048], P(('seq', 'section')), may hold values from -3 to 0
- a_log: float32 [2048, 8], P(('seq', 'section')), may hold values from -7 to 0
- skip_gain: float32 [2048], P(('seq', 'section')), may hold values from -2.5 to 2.5
Outputs:
- mixer_out: bfloat16 [2048, 1024], P(('seq', 'section'))
The draws below stay inside these ranges and needn't reach their ends.
All inputs are finite; a program needn't handle non-finite values.
Results may differ from the reference program's by a relative error of at most 0.03.
Values may be sent and summed in bfloat16 or wider, within the bound.
No kernel may reach another device: no remote copies, remote signals or barrier semaphores. Data moves between devices by JAX's collectives and lax.ppermute only.
A program may use at most 128 MiB of HBM per device.

```python
import math
import jax
import jax.numpy as jnp
from jax import lax

D = 8192
HD = 128
GROUP = 4
KVH = 4
HQ = 16
NST = 8
DT_RANK = 256
CONV = 4
E = 2048
L = 1024
N_SEQ = 8


def drawn_pair(key):
    query_key = jax.random.fold_in(key, 101)
    key_key = jax.random.fold_in(key, 202)
    query_base = jnp.clip(jax.random.normal(query_key, (L, KVH, GROUP, HD), jnp.float32), -6.0, 6.0)
    key_base = jnp.clip(jax.random.normal(key_key, (L, KVH, HD), jnp.float32), -6.0, 6.0)
    return (query_base.reshape(L, KVH * GROUP * HD), key_base.reshape(L, KVH * HD))


def draw_queries(key, part):
    return drawn_pair(key)[0].astype(jnp.bfloat16)


def draw_keys(key, part):
    return drawn_pair(key)[1].astype(jnp.bfloat16)


def draw_residual(key, part):
    column_scale = 10.0 ** (jnp.arange(D, dtype=jnp.float32) / D)
    base = jnp.clip(jax.random.normal(jax.random.fold_in(key, 1), (L, D), jnp.float32), -4.0, 4.0)
    row_scale = 10.0 ** jax.random.uniform(jax.random.fold_in(key, 3), (L,), jnp.float32, 0.0, 1.0)
    return (0.01 * base * row_scale[:, None] * column_scale[None, :]).astype(jnp.bfloat16)


def with_spikes(values, rng, source, target, parts, factor):
    def block_of(dim):
        return (jnp.arange(values.shape[dim]) // (values.shape[dim] // parts)).reshape((-1,) + (1,) * (values.ndim - 1 - dim))

    first = jax.random.permutation(rng, parts)[block_of(target)]
    other_side = (block_of(target) + parts // 2) % parts
    return jnp.where((block_of(source) == first) | (block_of(source) == other_side), factor * values, values)


def level_of(key, shape, split, low, high):
    loudness = 1.0
    for axis_at, blocks in split:
        steps = jax.random.uniform(jax.random.fold_in(jax.random.fold_in(key, 6), axis_at), (blocks,), jnp.float32, low / len(split), high / len(split))
        loudness = loudness * jnp.repeat(jnp.exp(steps), shape[axis_at] // blocks).reshape((-1,) + (1,) * (len(shape) - 1 - axis_at))
    return loudness


def bell_draw(own_key, shape, deviation, limit, split=(), kind=jnp.bfloat16):
    factor_of = level_of(own_key, shape, split, -0.22, 0.18) if split else 1.0
    drawn = jax.random.normal(own_key, shape, jnp.float32) * deviation * factor_of
    return jnp.minimum(jnp.maximum(drawn, -limit), limit).astype(kind)


def bell_draw_with(stream_key, dims, scale, limit, cuts, heavy, kind=jnp.bfloat16):
    values = scale * jax.random.normal(stream_key, dims, jnp.float32)
    if cuts:
        values = values * level_of(stream_key, dims, cuts, -0.22, 0.18)
    return jnp.clip(with_spikes(values, jax.random.fold_in(stream_key, 3), *heavy), -limit, limit).astype(kind)


def setup_inputs(seed: int = 0) -> dict:
    key_of = jax.random.split(jax.random.key(seed), 15)
    queries = draw_queries(jax.random.fold_in(key_of[14], 71), 0)
    keys = draw_keys(jax.random.fold_in(key_of[14], 71), 0)
    values = bell_draw(key_of[2], (L, KVH * HD), 3.0, 18.0, ((0, 8), (1, 4)))
    residual = draw_residual(jax.random.fold_in(key_of[14], 71), 0)
    out_weight = bell_draw(key_of[4], (HQ * HD, D), (HQ * HD) ** -0.5, 0.125, ((0, 4), (1, 8)))
    norm_gain = jnp.clip(1.0 + 0.18 * jax.random.normal(key_of[5], (D,), jnp.float32), 0.1, 1.9)
    in_weight = bell_draw_with(key_of[6], (D, 2, N_SEQ, E // N_SEQ), D ** -0.5, 0.09375, ((0, 8), (3, 4)), (0, 2, 8, 2.0))
    conv_weight = bell_draw(key_of[7], (E, CONV), 0.5, 3.0, ((0, 32),), jnp.float32)
    conv_bias = jnp.clip(jax.random.uniform(key_of[8], (E,), jnp.float32, -0.5, 0.5) * level_of(key_of[8], (E,), ((0, 32),), -0.4, 0.0), -0.5, 0.5)
    proj_weight = bell_draw(key_of[9], (E, DT_RANK + 2 * NST), E ** -0.5, 0.125, ((0, 32),))
    dt_weight = bell_draw(key_of[10], (DT_RANK, E), DT_RANK ** -0.5, 0.375, ((1, 32),))
    dt_bias = jnp.clip(-3.0 + 3.0 * jax.random.uniform(key_of[11], (E,), jnp.float32) ** level_of(key_of[11], (E,), ((0, 32),), -0.2, 0.2), -3.0, 0.0)
    a_log = jnp.clip(-7.0 + 7.0 * jax.random.uniform(key_of[12], (E, NST), jnp.float32) ** level_of(key_of[12], (E, NST), ((0, 32),), -0.2, 0.2), -7.0, 0.0)
    skip_gain = jnp.clip(jax.random.uniform(key_of[13], (E,), jnp.float32, -2.5, 2.5) * level_of(key_of[13], (E,), ((0, 32),), -0.4, 0.0), -2.5, 2.5)
    return dict(queries=queries, keys=keys, values=values, residual=residual, out_weight=out_weight, norm_gain=norm_gain, in_weight=in_weight, conv_weight=conv_weight, conv_bias=conv_bias, proj_weight=proj_weight, dt_weight=dt_weight, dt_bias=dt_bias, a_log=a_log, skip_gain=skip_gain)


def attend_group(operands):
    query_group, key_rows, value_rows = operands
    scores = jnp.einsum('pgd,rd->gpr', query_group.astype(jnp.float32), key_rows.astype(jnp.float32)) / math.sqrt(HD)
    position = jnp.arange(L)
    allowed = (position[:, None] >= position[None, :])[None]
    scores = jnp.where(allowed, scores, -jnp.inf)
    row_max = lax.optimization_barrier(jnp.max(scores, axis=2, keepdims=True))
    exponent_terms = jnp.where(allowed, jnp.exp(scores - row_max), jnp.float32(0.0))
    weight_sum = lax.optimization_barrier(jnp.sum(exponent_terms, axis=2))
    weights_bf = exponent_terms.astype(jnp.bfloat16)
    summed = jnp.einsum('gpr,rd->pgd', weights_bf.astype(jnp.float32), value_rows.astype(jnp.float32))
    return (summed / jnp.transpose(weight_sum)[:, :, None]).astype(jnp.bfloat16)

def reference(queries, keys, values, residual, out_weight, norm_gain, in_weight, conv_weight, conv_bias, proj_weight, dt_weight, dt_bias, a_log, skip_gain):
    query_groups = jnp.transpose(queries.reshape(L, KVH, GROUP, HD), (1, 0, 2, 3))
    key_groups = jnp.transpose(keys.reshape(L, KVH, HD), (1, 0, 2))
    value_groups = jnp.transpose(values.reshape(L, KVH, HD), (1, 0, 2))
    attended = lax.map(attend_group, (query_groups, key_groups, value_groups))
    attended = jnp.transpose(attended, (1, 0, 2, 3)).reshape(L, HQ * HD)
    hidden = residual.astype(jnp.float32) + jnp.dot(attended, out_weight, preferred_element_type=jnp.float32)
    inv_rms = lax.rsqrt(lax.optimization_barrier(jnp.sum(hidden * hidden, axis=1)) / D + 1e-05)
    normed = (hidden * inv_rms[:, None] * norm_gain[None, :]).astype(jnp.bfloat16)
    weight_flat = in_weight.reshape(D, 2, E)
    width = D // N_SEQ

    def add_block(block_index, running):
        begin = (block_index * width).astype(jnp.int32)
        rows = lax.dynamic_slice_in_dim(normed, begin, width, 1)
        block_weight = lax.dynamic_slice_in_dim(weight_flat, begin, width, 0)
        partial_sum = jnp.einsum('ld,dke->kel', rows.astype(jnp.float32), block_weight.astype(jnp.float32))
        rounded = lax.optimization_barrier(partial_sum.astype(jnp.bfloat16))
        return running + rounded.astype(jnp.float32)
    mixed_in = lax.fori_loop(jnp.int32(0), jnp.int32(N_SEQ), add_block, jnp.zeros((2, E, L), jnp.float32))
    x_path = mixed_in[0]
    z_gate = mixed_in[1]
    padded = jnp.pad(x_path, ((0, 0), (CONV - 1, 0)))
    conv_out = conv_bias[:, None] + jnp.zeros((E, L), jnp.float32)
    for offset in range(CONV):
        conv_out = conv_out + conv_weight[:, offset:offset + 1] * padded[:, offset:offset + L]
    inputs = jax.nn.silu(conv_out).astype(jnp.bfloat16)
    projected = jnp.dot(jnp.transpose(proj_weight), inputs, preferred_element_type=jnp.float32)
    low_rank = projected[:DT_RANK].astype(jnp.bfloat16)
    in_map = projected[DT_RANK:DT_RANK + NST]
    out_map = projected[DT_RANK + NST:]
    step_size = jax.nn.softplus(jnp.dot(jnp.transpose(dt_weight), low_rank, preferred_element_type=jnp.float32) + dt_bias[:, None])
    decay = -jnp.exp(a_log)
    inputs_float = inputs.astype(jnp.float32)

    def advance(carried, column):
        step_col, input_col, in_col, out_col = column
        carried = jnp.exp(step_col[:, None] * decay) * carried + (step_col * input_col)[:, None] * in_col[None, :]
        return (carried, lax.optimization_barrier(jnp.sum(carried * out_col[None, :], axis=1)))
    columns = (jnp.transpose(step_size), jnp.transpose(inputs_float), jnp.transpose(in_map), jnp.transpose(out_map))
    final_state, outputs = lax.scan(advance, jnp.zeros((E, NST), jnp.float32), columns)
    readout = jnp.transpose(outputs)
    return ((readout + skip_gain[:, None] * inputs_float) * jax.nn.silu(z_gate)).astype(jnp.bfloat16)
```

```python
import functools
import math

import jax
import jax.numpy as jnp
from jax import lax
from jax.experimental import pallas as pl
from jax.experimental.pallas import tpu as pltpu
from jax.sharding import PartitionSpec as P

D = 8192
HD = 128
GROUP = 4
NST = 8
DT_RANK = 256
CONV = 4
NORM_EPS = 1e-05
HALO = 16
VMEM_LIMIT = 56 * 1024 * 1024

F32 = jnp.float32
BF16 = jnp.bfloat16

NN = (((1,), (0,)), ((), ()))
NT = (((1,), (1,)), ((), ()))
TN = (((0,), (0,)), ((), ()))


def dot(lhs, rhs, dims=NN):
    return lax.dot_general(lhs, rhs, dims, preferred_element_type=F32)


def call(kernel, out_shape, n_in, scratch=(), flops=0, size=0, in_place=None, out_place=pltpu.VMEM):
    in_place = in_place or [pltpu.VMEM] * n_in
    return pl.pallas_call(
        kernel,
        out_shape=out_shape,
        in_specs=[pl.BlockSpec(memory_space=place) for place in [pltpu.SMEM] + in_place],
        out_specs=jax.tree.map(lambda _: pl.BlockSpec(memory_space=out_place), out_shape),
        scratch_shapes=list(scratch),
        compiler_params=pltpu.CompilerParams(vmem_limit_bytes=VMEM_LIMIT),
        cost_estimate=pl.CostEstimate(flops=flops, bytes_accessed=size, transcendentals=0),
    )


def swap(x, axis, count, bits):
    return lax.ppermute(x, axis, [(i, i ^ bits) for i in range(count)])


def after(x, *others):
    return lax.optimization_barrier((x, *others))[0]


def gather_seq(messages, count, *others):
    even = [messages[0]] + [swap(messages[k // 2], "seq", count, k) for k in range(2, count, 2)]
    even, others = lax.optimization_barrier((even, others))
    pieces = []
    for piece in even:
        pieces += [piece, swap(piece, "seq", count, 1)]
    return pieces, others


def attention_kernel(count, rank_ref, query_ref, *refs):
    kv_refs = refs[:count]
    out_ref, scores_ref, value_ref = refs[count:]
    rank = rank_ref[0]
    rows = query_ref.shape[0]
    stacked = jnp.concatenate(
        [query_ref[:, g * HD : (g + 1) * HD] for g in range(GROUP)], axis=0
    )
    maxima = None
    for k in range(count):
        part = dot(stacked, kv_refs[k][:, :HD], NT) * (1.0 / math.sqrt(HD))
        if k == 0:
            row = lax.broadcasted_iota(jnp.int32, part.shape, 0) % rows
            col = lax.broadcasted_iota(jnp.int32, part.shape, 1)
            part = jnp.where(row >= col, part, -1e30)
        else:
            earlier = jnp.bitwise_xor(rank, k) < rank
            part = jnp.where(earlier, part, -1e30)
        scores_ref[:, k * rows : (k + 1) * rows] = part
        value_ref[k * rows : (k + 1) * rows, :] = kv_refs[k][:, HD:]
        peak = jnp.max(part, axis=1, keepdims=True)
        maxima = peak if maxima is None else jnp.maximum(maxima, peak)
    terms = jnp.exp(scores_ref[...] - maxima)
    total = jnp.sum(terms, axis=1, keepdims=True)
    result = dot(terms.astype(BF16), value_ref[...]) / total
    result = result.astype(BF16)
    for g in range(GROUP):
        out_ref[:, g * HD : (g + 1) * HD] = result[g * rows : (g + 1) * rows, :]


class Copies:
    def __init__(self, semaphores):
        self.semaphores = semaphores
        self.count = 0

    def start(self, source, target):
        copy = pltpu.make_async_copy(source, target, self.semaphores.at[self.count])
        self.count += 1
        copy.start()
        return copy


def own_kernel(count, rank_ref, *refs):
    own_refs = refs[:count]
    weight_ref, residual_ref, acc_ref, left_ref = refs[count:]
    rank = rank_ref[0]
    rows = own_refs[0].shape[0]
    for k in range(count):
        left_ref[k * rows : (k + 1) * rows, :] = own_refs[k][...]
    tile = 2 * rows
    for t in range(count // 2):
        total = dot(left_ref[t * tile : (t + 1) * tile, :], weight_ref[...])
        for half in range(2):
            k = 2 * t + half
            first = pl.multiple_of(jnp.bitwise_xor(rank, k) * rows, rows)
            acc_ref[k * rows : (k + 1) * rows, :] = total[
                half * rows : (half + 1) * rows
            ] + residual_ref[pl.ds(first, rows), :].astype(F32)


def mix_kernel(count, used, rank_ref, *refs):
    far_refs = refs[:count]
    weight_refs = refs[count : count + used]
    refs = refs[count + used :]
    acc_ref, gain_ref, in_ref = refs[:3]
    out_refs = refs[3 : count + 3]
    left, weights, acc, columns, normed, mixed, halos, squares, semaphores = refs[count + 3 :]
    rank = rank_ref[0]
    rows = far_refs[0].shape[0]
    width = weight_refs[0].shape[0]
    channels = in_ref.shape[1]
    copies = Copies(semaphores)
    weight_copies = [
        copies.start(weight_refs[r], weights.at[pl.ds(r * width, width), :]) for r in range(used)
    ]
    tile = rows * count // 2
    left_copies, acc_copies, out_copies = [], [], []
    for t in range(2):
        left_copies.append(
            [
                copies.start(
                    far_refs[k],
                    left.at[pl.ds(k * rows, rows), :],
                )
                for k in range(t * count // 2, (t + 1) * count // 2)
            ]
        )
        span = pl.ds(t * tile, tile)
        acc_copies.append(copies.start(acc_ref.at[span, :], acc.at[span, :]))
    column_copy = copies.start(in_ref, columns)
    for copy in weight_copies:
        copy.wait()
    eye = lax.broadcasted_iota(jnp.int32, (rows, rows), 0) == lax.broadcasted_iota(
        jnp.int32, (rows, rows), 1
    )
    for t in range(2):
        span = pl.ds(t * tile, tile)
        for copy in left_copies[t]:
            copy.wait()
        total = dot(left[span, :], weights[...])
        acc_copies[t].wait()
        hidden = acc[span, :] + total
        normed[span, :] = (hidden * gain_ref[...]).astype(BF16)
        sums = jnp.sum(hidden * hidden, axis=1, keepdims=True)
        for part in range(count // 2):
            k = t * count // 2 + part
            squares[k : k + 1, :] = jnp.sum(
                jnp.where(eye, sums[part * rows : (part + 1) * rows], 0.0),
                axis=0,
                keepdims=True,
            )
    column_copy.wait()
    for t in range(2):
        result = dot(normed[pl.ds(t * tile, tile), :], columns[...]).astype(BF16)
        mixed[pl.ds(t * tile, tile), :] = result
        for part in range(count // 2):
            k = t * count // 2 + part
            out_copies.append(
                copies.start(
                    mixed.at[pl.ds(k * rows, rows), :], out_refs[k].at[pl.ds(HALO, rows), :]
                )
            )
    line = lax.broadcasted_iota(jnp.int32, (HALO, channels), 0)
    for k in range(count):
        block = jnp.bitwise_xor(rank, k)
        before = jnp.bitwise_xor(rank, jnp.maximum(block - 1, 0))
        last = pl.multiple_of(before * rows + (rows - HALO), HALO)
        halo = mixed[pl.ds(last, HALO), :].astype(F32)
        own = jnp.tile(squares[k : k + 1, :], (1, channels // rows))
        past = jnp.tile(squares[pl.ds(before, 1), :], (1, channels // rows))
        halo = jnp.where(line == 0, own, jnp.where(line == 1, past, halo))
        halos[k] = halo.astype(BF16)
        out_copies.append(copies.start(halos.at[k], out_refs[k].at[pl.ds(0, HALO), :]))
    for copy in out_copies:
        copy.wait()


def conv_kernel(n_pieces, count, rank_ref, *refs):
    piece_refs = refs[:n_pieces]
    param_refs = refs[n_pieces : n_pieces + count]
    out_ref, maps_ref, total_ref = refs[n_pieces + count :]
    rank = rank_ref[0]
    total = piece_refs[0][...].astype(F32)
    for piece in piece_refs[1:]:
        total += piece[...].astype(F32)
    rows = total.shape[0] - HALO
    eye = lax.broadcasted_iota(jnp.int32, (rows, rows), 0) == lax.broadcasted_iota(
        jnp.int32, (rows, rows), 1
    )
    scale_own = lax.rsqrt(total[0:1, :rows] / D + NORM_EPS)
    scale_past = lax.rsqrt(total[1:2, :rows] / D + NORM_EPS)
    scale_past = jnp.where(rank == 0, 0.0, scale_past)
    column_own = jnp.sum(jnp.where(eye, scale_own, 0.0), axis=1, keepdims=True)
    column_past = jnp.sum(jnp.where(eye, scale_past, 0.0), axis=1, keepdims=True)
    total_ref[0:8, :] = total[HALO - 8 : HALO] * column_past[rows - 8 :]
    total_ref[8:, :] = total[HALO:] * column_own
    group = out_ref.shape[2]
    middle = DT_RANK + 2 * NST
    projected = jnp.zeros((middle, rows), F32)
    for k in range(count):
        first = pl.multiple_of(jnp.bitwise_xor(rank, k) * group, group)
        path = total_ref[:, pl.ds(first, group)]
        params = param_refs[k][middle:, :].astype(F32)
        taps = params[0:5] + params[5:10] + params[10:15]
        conv = taps[CONV : CONV + 1] + jnp.zeros((rows, group), F32)
        for offset in range(CONV):
            begin = 8 - (CONV - 1) + offset
            conv += taps[offset : offset + 1] * path[begin : begin + rows]
        result = (conv / (1.0 + jnp.exp(-conv))).astype(BF16)
        out_ref[k] = result
        projected += dot(param_refs[k][0:middle, :], result, NT)
    low_rank = projected[:DT_RANK]
    maps = projected[DT_RANK:]
    high = maps.astype(BF16)
    maps_ref[0:DT_RANK, :] = low_rank.astype(BF16)
    maps_ref[DT_RANK:middle, :] = high
    maps_ref[middle:, :] = (maps - high.astype(F32)).astype(BF16)


def sum_kernel(n_pieces, rank_ref, *refs):
    del rank_ref
    pairs_ref = refs[n_pieces]
    out_refs = refs[n_pieces + 1 :]
    rows = pairs_ref.shape[1]
    total = refs[0][...].astype(F32)
    for piece in refs[1:n_pieces]:
        total += piece[...].astype(F32)
    middle = DT_RANK + 2 * NST
    maps = total[DT_RANK:middle] + total[middle:]
    high = maps.astype(BF16)
    low = (maps - high.astype(F32)).astype(BF16)
    low_rank = total[:DT_RANK].astype(BF16)
    for at, out_ref in enumerate(out_refs):
        out_ref[0:rows, :] = pairs_ref[2 * at]
        out_ref[rows : 2 * rows, :] = pairs_ref[2 * at + 1]
        out_ref[2 * rows : 2 * rows + DT_RANK, :] = low_rank
        out_ref[2 * rows + DT_RANK : 2 * rows + middle, :] = high
        out_ref[2 * rows + middle :, :] = low


def scan_kernel(count, rank_ref, *refs):
    rows = (refs[0].shape[0] - DT_RANK - 4 * NST) // 2
    pair_refs = [refs[k].at[pl.ds(k % 2 * rows, rows), :] for k in range(count)]
    maps_refs = [refs[k].at[pl.ds(2 * rows, DT_RANK + 4 * NST), :] for k in range(count)]
    (
        weight_ref, bias_ref, decay_ref, skip_ref, out_ref,
        factor_ref, source_ref, read_ref, value_ref, end_ref, product_ref, begin_ref,
    ) = refs[count:]
    rank = rank_ref[0]
    lanes = weight_ref.shape[1]
    half = lanes // 2
    groups = NST // 2
    wide = groups * lanes
    map_rows = maps_refs[0].shape[0] - DT_RANK
    map_row = lax.broadcasted_iota(jnp.int32, (map_rows, wide), 0) % (2 * NST)
    state_of = lax.broadcasted_iota(jnp.int32, (map_rows, wide), 1) // half
    spread_in = jnp.where(map_row == state_of, 1.0, 0.0).astype(BF16)
    spread_out = jnp.where(map_row == state_of + NST, 1.0, 0.0).astype(BF16)
    lane = lax.broadcasted_iota(jnp.int32, (rows, lanes), 1)
    for k in range(count):
        span = slice(k * rows, (k + 1) * rows)
        step = dot(maps_refs[k][:DT_RANK, :], weight_ref[...], TN) + bias_ref[...]
        step = jnp.maximum(step, 0.0) + jnp.log1p(jnp.exp(-jnp.abs(step)))
        pair = pair_refs[k][...].astype(F32)
        value = jnp.where(lane < half, pair, pltpu.roll(pair, half, 1))
        value_ref[span, :] = value
        maps = maps_refs[k][DT_RANK:, :]
        in_map = dot(maps, spread_in, TN)
        read_ref[span, :] = dot(maps, spread_out, TN)
        drive = step * value
        for g in range(groups):
            part = slice(g * lanes, (g + 1) * lanes)
            factor_ref[g, span, :] = jnp.exp(step * decay_ref[:, part])
            source_ref[g, span, :] = drive * in_map[:, part]

    def advance(t, carried):
        at = pl.ds(t, count, stride=rows)
        following = []
        for g in range(groups):
            state, product = carried[g]
            factor = factor_ref[g, at, :]
            state = factor * state + source_ref[g, at, :]
            product = factor * product
            source_ref[g, at, :] = state
            factor_ref[g, at, :] = product
            following.append((state, product))
        return following

    carried = lax.fori_loop(
        0,
        rows,
        advance,
        [(jnp.zeros((count, lanes), F32), jnp.ones((count, lanes), F32))] * groups,
        unroll=8,
    )
    state = jnp.concatenate([pair[0] for pair in carried], axis=1)
    product = jnp.concatenate([pair[1] for pair in carried], axis=1)
    end_ref[...] = state
    product_ref[...] = product
    carried = jnp.zeros((1, wide), F32)
    for j in range(count):
        at = pl.ds(jnp.bitwise_xor(rank, j), 1)
        begin_ref[at, :] = carried
        carried = product_ref[at, :] * carried + end_ref[at, :]
    for k in range(count):
        span = slice(k * rows, (k + 1) * rows)
        total = skip_ref[...] * value_ref[span, :]
        readout = jnp.zeros((rows, lanes), F32)
        for g in range(groups):
            part = slice(g * lanes, (g + 1) * lanes)
            state = source_ref[g, span, :] + factor_ref[g, span, :] * begin_ref[k : k + 1, part]
            readout += state * read_ref[span, part]
        total += readout + pltpu.roll(readout, half, 1)
        result = jnp.transpose(total * pair_refs[k][...].astype(F32))
        first = pl.multiple_of(jnp.bitwise_xor(rank, k) * rows, rows)
        out_ref[:, pl.ds(first, rows)] = result[half:].astype(BF16)


def body(
    n_seq,
    n_sec,
    queries,
    keys,
    values,
    residual,
    out_weight,
    norm_gain,
    in_weight,
    conv_weight,
    conv_bias,
    proj_weight,
    dt_weight,
    dt_bias,
    a_log,
    skip_gain,
):
    shape = jax.ShapeDtypeStruct
    rows = queries.shape[0]
    seq_len = residual.shape[0]
    features = residual.shape[1]
    own = conv_weight.shape[0]
    channels = n_seq * 2 * own
    rank = lax.axis_index("seq").astype(jnp.int32)
    rank_arg = rank.reshape(1)

    others_at = list(range(1, n_sec))
    far_at = list(range(3, n_sec, 2))
    weights = {r: swap(out_weight, "section", n_sec, r) for r in far_at}

    pairs, _ = gather_seq([jnp.concatenate([keys, values], axis=1)] * (n_seq // 2), n_seq)
    attended = call(
        functools.partial(attention_kernel, n_seq),
        shape((rows, GROUP * HD), BF16),
        1 + n_seq,
        [pltpu.VMEM((GROUP * rows, seq_len), F32), pltpu.VMEM((seq_len, HD), BF16)],
        flops=4 * GROUP * rows * seq_len * HD,
        size=4 * rows * 4 * HD * n_seq,
    )(rank_arg, queries, *pairs)

    far = jnp.concatenate(
        [swap(attended, "section", n_sec, r) for r in others_at], axis=1
    )
    own_pieces, _ = gather_seq([attended] * (n_seq // 2), n_seq)
    nearest = swap(after(out_weight, own_pieces[-1]), "section", n_sec, 1)
    for r in range(2, n_sec, 2):
        weights[r] = swap(after(weights[r + 1], far), "section", n_sec, 1)

    width = out_weight.shape[0]
    conv = jnp.concatenate([conv_weight, conv_bias[:, None]], axis=1).T
    identity = jnp.zeros_like(conv).at[CONV - 1].set(1.0)
    conv = jnp.concatenate([conv, identity], axis=1)
    terms = []
    for _ in range(3):
        high = lax.reduce_precision(conv, 8, 7)
        terms.append(high.astype(BF16))
        conv = conv - high
    proj = jnp.concatenate([proj_weight, jnp.zeros_like(proj_weight)], axis=0).reshape(
        2, own, -1
    )
    proj = jnp.transpose(proj, (2, 0, 1)).reshape(-1, 2 * own)
    params = jnp.concatenate([proj, *terms, jnp.zeros((1, 2 * own), BF16)], axis=0)
    params, _ = gather_seq([after(params, attended)] * (n_seq // 2), n_seq)
    in_columns = jnp.transpose(in_weight, (0, 2, 1, 3)).reshape(features, channels)
    far = after(far, in_columns)

    acc = call(
        functools.partial(own_kernel, n_seq),
        shape((seq_len, features), F32),
        n_seq + 2,
        [pltpu.VMEM((seq_len, width), BF16)],
        flops=2 * seq_len * features * width,
        size=seq_len * features * 8,
    )(rank_arg, *own_pieces, out_weight, residual)
    far_pieces, others = gather_seq(
        [far] * (n_seq // 2),
        n_seq,
        acc, nearest, *params,
    )
    acc, weights[1], *params = others
    used = n_sec - 1
    payloads = call(
        functools.partial(mix_kernel, n_seq, used),
        [shape((HALO + rows, channels), BF16)] * n_seq,
        n_seq + used + 3,
        [
            pltpu.VMEM((seq_len, width * used), BF16),
            pltpu.VMEM((used * width, features), BF16),
            pltpu.VMEM((seq_len, features), F32),
            pltpu.VMEM((features, channels), BF16),
            pltpu.VMEM((seq_len, features), BF16),
            pltpu.VMEM((seq_len, channels), BF16),
            pltpu.VMEM((n_seq, HALO, channels), BF16),
            pltpu.VMEM((n_seq, rows), F32),
            pltpu.SemaphoreType.DMA((3 * n_seq + 2 * used + 3,)),
        ],
        flops=2 * seq_len * features * (width * used + channels),
        size=seq_len * features * 12,
        in_place=[pl.ANY] * (n_seq + used + 1) + [pltpu.VMEM, pl.ANY],
        out_place=pl.ANY,
    )(
        rank_arg,
        *far_pieces,
        *[weights[r] for r in others_at],
        acc,
        norm_gain.reshape(1, -1),
        in_columns,
    )

    arrived = {k: swap(payloads[k], "seq", n_seq, 1) for k in range(n_seq - 1, 0, -2)}
    summed = {
        k: (payloads[k].astype(F32) + arrived[k + 1].astype(F32)).astype(BF16)
        for k in range(0, n_seq, 2)
    }
    pieces = [summed[0]] + [swap(summed[k], "seq", n_seq, k) for k in range(2, n_seq, 2)]

    map_rows = DT_RANK + 4 * NST
    outgoing, maps = call(
        functools.partial(conv_kernel, len(pieces), n_seq),
        [shape((n_seq, rows, 2 * own), BF16), shape((map_rows, rows), BF16)],
        len(pieces) + n_seq,
        [pltpu.VMEM((rows + 8, channels), F32)],
        flops=2 * rows * channels * map_rows,
        size=rows * channels * 12,
    )(rank_arg, *pieces, *params)

    map_parts = [maps] + [swap(maps, "section", n_sec, r) for r in range(1, n_sec)]
    messages = call(
        functools.partial(sum_kernel, n_sec),
        [shape((2 * rows + map_rows, rows), BF16)] * (n_seq // 2),
        n_sec + 1,
        size=map_rows * rows * 2 * n_sec,
    )(rank_arg, *map_parts, outgoing)
    scan_pieces, _ = gather_seq(messages, n_seq)

    weight = jnp.concatenate([dt_weight, dt_weight], axis=1)
    bias = jnp.concatenate([dt_bias, dt_bias]).reshape(1, -1)
    skip = jnp.concatenate([skip_gain, skip_gain]).reshape(1, -1)
    decay = (-jnp.exp(a_log)).T.reshape(1, -1)
    wide = NST * own
    return call(
        functools.partial(scan_kernel, n_seq),
        shape((own, seq_len), BF16),
        n_seq + 4,
        [pltpu.VMEM((NST // 2, seq_len, 2 * own), F32)] * 2
        + [pltpu.VMEM((seq_len, wide), F32)]
        + [pltpu.VMEM((seq_len, 2 * own), F32)]
        + [pltpu.VMEM((n_seq, wide), F32)] * 3,
        flops=2 * seq_len * DT_RANK * own,
        size=seq_len * wide * 8,
    )(rank_arg, *scan_pieces, weight, bias, decay, skip)


def solution(mesh):
    return jax.shard_map(
        functools.partial(body, mesh.shape["seq"], mesh.shape["section"]),
        mesh=mesh,
        in_specs=(
            P("seq", "section"),
            P("seq", "section"),
            P("seq", "section"),
            P(None, "seq"),
            P("section", "seq"),
            P("seq"),
            P("seq", None, None, "section"),
            P(("seq", "section"), None),
            P(("seq", "section")),
            P(("seq", "section"), None),
            P(None, ("seq", "section")),
            P(("seq", "section")),
            P(("seq", "section"), None),
            P(("seq", "section")),
        ),
        out_specs=P(("seq", "section"), None),
        check_vma=False,
    )
```

```python
import functools
import math

import jax
import jax.numpy as jnp
from jax import lax
from jax.experimental import pallas as pl
from jax.experimental.pallas import tpu as pltpu
from jax.sharding import PartitionSpec as P

D = 8192
HD = 128
GROUP = 4
NST = 8
DT_RANK = 256
CONV = 4
NORM_EPS = 1e-05
HALO = 16
PAD = 8
MIB = 1024 * 1024
VMEM_LIMIT = 56 * MIB

F32 = jnp.float32
BF16 = jnp.bfloat16

NN = (((1,), (0,)), ((), ()))
NT = (((1,), (1,)), ((), ()))
TN = (((0,), (0,)), ((), ()))


def dot(lhs, rhs, dims=NN):
    return lax.dot_general(lhs, rhs, dims, preferred_element_type=F32)


def call(kernel, out_shape, n_in, scratch=(), flops=0, size=0, in_place=None, out_place=pltpu.VMEM, limit=16):
    in_place = in_place or [pltpu.VMEM] * n_in
    return pl.pallas_call(
        kernel,
        out_shape=out_shape,
        in_specs=[pl.BlockSpec(memory_space=place) for place in [pltpu.SMEM] + in_place],
        out_specs=jax.tree.map(lambda _: pl.BlockSpec(memory_space=out_place), out_shape),
        scratch_shapes=list(scratch),
        compiler_params=pltpu.CompilerParams(vmem_limit_bytes=min(limit * MIB, VMEM_LIMIT)),
        cost_estimate=pl.CostEstimate(flops=flops, bytes_accessed=size, transcendentals=0),
    )


def swap(x, axis, count, bits):
    return lax.ppermute(x, axis, [(i, i ^ bits) for i in range(count)])


def after(x, *others):
    return lax.optimization_barrier((x, *others))[0]


def gather_seq(messages, count, *others):
    even = [messages[0]] + [swap(messages[k // 2], "seq", count, k) for k in range(2, count, 2)]
    even, others = lax.optimization_barrier((even, others))
    pieces = []
    for piece in even:
        pieces += [piece, swap(piece, "seq", count, 1)]
    return pieces, others


def attention_kernel(count, rank_ref, query_ref, *refs):
    kv_refs = refs[:count]
    out_ref, scores_ref, value_ref = refs[count:]
    rank = rank_ref[0]
    rows = query_ref.shape[0]
    stacked = jnp.concatenate(
        [query_ref[:, g * HD : (g + 1) * HD] for g in range(GROUP)], axis=0
    )
    maxima = None
    for k in range(count):
        part = dot(stacked, kv_refs[k][:, :HD], NT) * (1.0 / math.sqrt(HD))
        if k == 0:
            row = lax.broadcasted_iota(jnp.int32, part.shape, 0) % rows
            col = lax.broadcasted_iota(jnp.int32, part.shape, 1)
            part = jnp.where(row >= col, part, -1e30)
        else:
            earlier = jnp.bitwise_xor(rank, k) < rank
            part = jnp.where(earlier, part, -1e30)
        scores_ref[:, k * rows : (k + 1) * rows] = part
        value_ref[k * rows : (k + 1) * rows, :] = kv_refs[k][:, HD:]
        peak = jnp.max(part, axis=1, keepdims=True)
        maxima = peak if maxima is None else jnp.maximum(maxima, peak)
    terms = jnp.exp(scores_ref[...] - maxima)
    total = jnp.sum(terms, axis=1, keepdims=True)
    result = dot(terms.astype(BF16), value_ref[...]) / total
    result = result.astype(BF16)
    for g in range(GROUP):
        out_ref[:, g * HD : (g + 1) * HD] = result[g * rows : (g + 1) * rows, :]


class Copies:
    def __init__(self, semaphores):
        self.semaphores = semaphores
        self.count = 0

    def start(self, source, target):
        copy = pltpu.make_async_copy(source, target, self.semaphores.at[self.count])
        self.count += 1
        copy.start()
        return copy


def own_kernel(count, rank_ref, *refs):
    own_refs = refs[:count]
    weight_ref, residual_ref, acc_ref, left_ref = refs[count:]
    rank = rank_ref[0]
    rows = own_refs[0].shape[0]
    for k in range(count):
        left_ref[k * rows : (k + 1) * rows, :] = own_refs[k][...]
    tile = 2 * rows
    for t in range(count // 2):
        total = dot(left_ref[t * tile : (t + 1) * tile, :], weight_ref[...])
        for half in range(2):
            k = 2 * t + half
            first = pl.multiple_of(jnp.bitwise_xor(rank, k) * rows, rows)
            acc_ref[k * rows : (k + 1) * rows, :] = total[
                half * rows : (half + 1) * rows
            ] + residual_ref[pl.ds(first, rows), :].astype(F32)


def mix_kernel(count, used, rank_ref, *refs):
    far_refs = refs[:count]
    weight_refs = refs[count : count + used]
    refs = refs[count + used :]
    acc_ref, gain_ref, in_ref = refs[:3]
    out_refs = refs[3 : count + 3]
    left, weights, acc, columns, normed, mixed, halos, squares, semaphores = refs[count + 3 :]
    rank = rank_ref[0]
    rows = far_refs[0].shape[0]
    width = weight_refs[0].shape[0]
    channels = in_ref.shape[0]
    copies = Copies(semaphores)
    weight_copies = [
        copies.start(weight_refs[r], weights.at[pl.ds(r * width, width), :]) for r in range(used)
    ]
    tile = rows * count // 2
    left_copies, acc_copies, out_copies = [], [], []
    for t in range(2):
        left_copies.append(
            [
                copies.start(
                    far_refs[k],
                    left.at[pl.ds(k * rows, rows), :],
                )
                for k in range(t * count // 2, (t + 1) * count // 2)
            ]
        )
        span = pl.ds(t * tile, tile)
        acc_copies.append(copies.start(acc_ref.at[span, :], acc.at[span, :]))
    column_copy = copies.start(in_ref, columns)
    for copy in weight_copies:
        copy.wait()
    eye = lax.broadcasted_iota(jnp.int32, (rows, rows), 0) == lax.broadcasted_iota(
        jnp.int32, (rows, rows), 1
    )
    for t in range(2):
        span = pl.ds(t * tile, tile)
        for copy in left_copies[t]:
            copy.wait()
        total = dot(left[span, :], weights[...])
        acc_copies[t].wait()
        hidden = acc[span, :] + total
        normed[span, :] = (hidden * gain_ref[...]).astype(BF16)
        sums = jnp.sum(hidden * hidden, axis=1, keepdims=True)
        for part in range(count // 2):
            k = t * count // 2 + part
            squares[k : k + 1, :] = jnp.sum(
                jnp.where(eye, sums[part * rows : (part + 1) * rows], 0.0),
                axis=0,
                keepdims=True,
            )
    column_copy.wait()
    for t in range(2):
        result = dot(normed[pl.ds(t * tile, tile), :], columns[...], NT).astype(BF16)
        mixed[pl.ds(t * tile, tile), :] = result
        for part in range(count // 2):
            k = t * count // 2 + part
            out_copies.append(
                copies.start(
                    mixed.at[pl.ds(k * rows, rows), :], out_refs[k].at[pl.ds(HALO, rows), :]
                )
            )
    line = lax.broadcasted_iota(jnp.int32, (HALO, channels), 0)
    for k in range(count):
        block = jnp.bitwise_xor(rank, k)
        before = jnp.bitwise_xor(rank, jnp.maximum(block - 1, 0))
        last = pl.multiple_of(before * rows + (rows - HALO), HALO)
        halo = mixed[pl.ds(last, HALO), :].astype(F32)
        own = jnp.tile(squares[k : k + 1, :], (1, channels // rows))
        past = jnp.tile(squares[pl.ds(before, 1), :], (1, channels // rows))
        halo = jnp.where(line == 0, own, jnp.where(line == 1, past, halo))
        halos[k] = halo.astype(BF16)
        out_copies.append(copies.start(halos.at[k], out_refs[k].at[pl.ds(0, HALO), :]))
    for copy in out_copies:
        copy.wait()


def conv_kernel(n_pieces, count, rank_ref, *refs):
    piece_refs = refs[:n_pieces]
    param_refs = refs[n_pieces : n_pieces + count]
    out_ref, maps_ref, total_ref = refs[n_pieces + count :]
    rank = rank_ref[0]
    total = piece_refs[0][...].astype(F32)
    for piece in piece_refs[1:]:
        total += piece[...].astype(F32)
    rows = total.shape[0] - HALO
    eye = lax.broadcasted_iota(jnp.int32, (rows, rows), 0) == lax.broadcasted_iota(
        jnp.int32, (rows, rows), 1
    )
    scale_own = lax.rsqrt(total[0:1, :rows] / D + NORM_EPS)
    scale_past = lax.rsqrt(total[1:2, :rows] / D + NORM_EPS)
    scale_past = jnp.where(rank == 0, 0.0, scale_past)
    column_own = jnp.sum(jnp.where(eye, scale_own, 0.0), axis=1, keepdims=True)
    column_past = jnp.sum(jnp.where(eye, scale_past, 0.0), axis=1, keepdims=True)
    total_ref[0:8, :] = total[HALO - 8 : HALO] * column_past[rows - 8 :]
    total_ref[8:, :] = total[HALO:] * column_own
    group = out_ref.shape[2]
    middle = DT_RANK + 2 * NST
    projected = jnp.zeros((middle, rows), F32)
    for k in range(count):
        first = pl.multiple_of(jnp.bitwise_xor(rank, k) * group, group)
        path = total_ref[:, pl.ds(first, group)]
        params = param_refs[k][middle:, :].astype(F32)
        taps = params[0:5] + params[5:10] + params[10:15]
        conv = taps[CONV : CONV + 1] + jnp.zeros((rows, group), F32)
        for offset in range(CONV):
            begin = 8 - (CONV - 1) + offset
            conv += taps[offset : offset + 1] * path[begin : begin + rows]
        result = (conv / (1.0 + jnp.exp(-conv))).astype(BF16)
        out_ref[k] = result
        projected += dot(param_refs[k][0:middle, :], result, NT)
    low_rank = projected[:DT_RANK]
    maps = projected[DT_RANK:]
    high = maps.astype(BF16)
    maps_ref[0:DT_RANK, :] = low_rank.astype(BF16)
    maps_ref[DT_RANK:middle, :] = high
    maps_ref[middle:, :] = (maps - high.astype(F32)).astype(BF16)


def sum_kernel(n_pieces, rank_ref, *refs):
    del rank_ref
    pairs_ref = refs[n_pieces]
    out_refs = refs[n_pieces + 1 :]
    rows = pairs_ref.shape[1]
    total = refs[0][...].astype(F32)
    for piece in refs[1:n_pieces]:
        total += piece[...].astype(F32)
    middle = DT_RANK + 2 * NST
    maps = total[DT_RANK:middle] + total[middle:]
    high = maps.astype(BF16)
    low = (maps - high.astype(F32)).astype(BF16)
    low_rank = total[:DT_RANK].astype(BF16)
    for at, out_ref in enumerate(out_refs):
        out_ref[0:rows, :] = pairs_ref[2 * at]
        out_ref[rows : 2 * rows, :] = pairs_ref[2 * at + 1]
        out_ref[2 * rows : 2 * rows + DT_RANK, :] = low_rank
        out_ref[2 * rows + DT_RANK : 2 * rows + middle, :] = high
        out_ref[2 * rows + middle :, :] = low


def scan_kernel(count, rank_ref, *refs):
    rows = (refs[0].shape[0] - DT_RANK - 4 * NST) // 2
    pair_refs = [refs[k].at[pl.ds(k % 2 * rows, rows), :] for k in range(count)]
    maps_refs = [refs[k].at[pl.ds(2 * rows, DT_RANK + 4 * NST), :] for k in range(count)]
    (
        weight_ref, bias_ref, decay_ref, skip_ref, out_ref,
        factor_ref, source_ref, read_ref, value_ref, end_ref, product_ref, begin_ref,
    ) = refs[count:]
    rank = rank_ref[0]
    pitch = rows + PAD
    lanes = weight_ref.shape[1]
    half = lanes // 2
    groups = NST // 2
    wide = groups * lanes
    map_rows = maps_refs[0].shape[0] - DT_RANK
    map_row = lax.broadcasted_iota(jnp.int32, (map_rows, wide), 0) % (2 * NST)
    state_of = lax.broadcasted_iota(jnp.int32, (map_rows, wide), 1) // half
    spread_in = jnp.where(map_row == state_of, 1.0, 0.0).astype(BF16)
    spread_out = jnp.where(map_row == state_of + NST, 1.0, 0.0).astype(BF16)
    lane = lax.broadcasted_iota(jnp.int32, (rows, lanes), 1)
    for k in range(count):
        span = slice(k * rows, (k + 1) * rows)
        padded = slice(k * pitch, k * pitch + rows)
        step = dot(maps_refs[k][:DT_RANK, :], weight_ref[...], TN) + bias_ref[...]
        step = jnp.maximum(step, 0.0) + jnp.log1p(jnp.exp(-jnp.abs(step)))
        pair = pair_refs[k][...].astype(F32)
        value = jnp.where(lane < half, pair, pltpu.roll(pair, half, 1))
        value_ref[span, :] = value
        maps = maps_refs[k][DT_RANK:, :]
        in_map = dot(maps, spread_in, TN)
        read_ref[span, :] = dot(maps, spread_out, TN)
        drive = step * value
        for g in range(groups):
            part = slice(g * lanes, (g + 1) * lanes)
            factor_ref[g, padded, :] = jnp.exp(step * decay_ref[:, part])
            source_ref[g, padded, :] = drive * in_map[:, part]

    def advance(t, carried):
        at = pl.ds(t, count, stride=pitch)
        following = []
        for g in range(groups):
            state, product = carried[g]
            factor = factor_ref[g, at, :]
            state = factor * state + source_ref[g, at, :]
            product = factor * product
            source_ref[g, at, :] = state
            factor_ref[g, at, :] = product
            following.append((state, product))
        return following

    carried = lax.fori_loop(
        0,
        rows,
        advance,
        [(jnp.zeros((count, lanes), F32), jnp.ones((count, lanes), F32))] * groups,
        unroll=8,
    )
    state = jnp.concatenate([pair[0] for pair in carried], axis=1)
    product = jnp.concatenate([pair[1] for pair in carried], axis=1)
    end_ref[...] = state
    product_ref[...] = product
    carried = jnp.zeros((1, wide), F32)
    for j in range(count):
        at = pl.ds(jnp.bitwise_xor(rank, j), 1)
        begin_ref[at, :] = carried
        carried = product_ref[at, :] * carried + end_ref[at, :]
    for k in range(count):
        span = slice(k * rows, (k + 1) * rows)
        padded = slice(k * pitch, k * pitch + rows)
        total = skip_ref[...] * value_ref[span, :]
        readout = jnp.zeros((rows, lanes), F32)
        for g in range(groups):
            part = slice(g * lanes, (g + 1) * lanes)
            state = source_ref[g, padded, :] + factor_ref[g, padded, :] * begin_ref[k : k + 1, part]
            readout += state * read_ref[span, part]
        total += readout + pltpu.roll(readout, half, 1)
        result = jnp.transpose(total * pair_refs[k][...].astype(F32))
        first = pl.multiple_of(jnp.bitwise_xor(rank, k) * rows, rows)
        out_ref[:, pl.ds(first, rows)] = result[half:].astype(BF16)


def scan_arguments(dt_weight, dt_bias, a_log, skip_gain):
    weight = jnp.concatenate([dt_weight, dt_weight], axis=1)
    bias = jnp.concatenate([dt_bias, dt_bias]).reshape(1, -1)
    skip = jnp.concatenate([skip_gain, skip_gain]).reshape(1, -1)
    decay = (-jnp.exp(a_log)).T.reshape(1, -1)
    return weight, bias, decay, skip


def body(
    n_seq,
    n_sec,
    queries,
    keys,
    values,
    residual,
    out_weight,
    norm_gain,
    in_weight,
    conv_weight,
    conv_bias,
    proj_weight,
    dt_weight,
    dt_bias,
    a_log,
    skip_gain,
):
    shape = jax.ShapeDtypeStruct
    rows = queries.shape[0]
    seq_len = residual.shape[0]
    features = residual.shape[1]
    scale = -(-seq_len // 1024)
    own = conv_weight.shape[0]
    channels = n_seq * 2 * own
    rank = lax.axis_index("seq").astype(jnp.int32)
    rank_arg = rank.reshape(1)

    others_at = list(range(1, n_sec))
    far_at = list(range(3, n_sec, 2))
    weights = {r: swap(out_weight, "section", n_sec, r) for r in far_at}

    pairs, _ = gather_seq([jnp.concatenate([keys, values], axis=1)] * (n_seq // 2), n_seq)
    attended = call(
        functools.partial(attention_kernel, n_seq),
        shape((rows, GROUP * HD), BF16),
        1 + n_seq,
        [pltpu.VMEM((GROUP * rows, seq_len), F32), pltpu.VMEM((seq_len, HD), BF16)],
        flops=4 * GROUP * rows * seq_len * HD,
        size=4 * rows * 4 * HD * n_seq,
        limit=16 * scale,
    )(rank_arg, queries, *pairs)

    far = jnp.concatenate(
        [swap(attended, "section", n_sec, r) for r in others_at], axis=1
    )
    own_pieces, _ = gather_seq([attended] * (n_seq // 2), n_seq)
    nearest = swap(after(out_weight, own_pieces[-1]), "section", n_sec, 1)
    for r in range(2, n_sec, 2):
        weights[r] = swap(after(weights[r + 1], far), "section", n_sec, 1)

    width = out_weight.shape[0]
    conv = jnp.concatenate([conv_weight, conv_bias[:, None]], axis=1).T
    identity = jnp.zeros_like(conv).at[CONV - 1].set(1.0)
    conv = jnp.concatenate([conv, identity], axis=1)
    terms = []
    for _ in range(3):
        high = lax.reduce_precision(conv, 8, 7)
        terms.append(high.astype(BF16))
        conv = conv - high
    proj = jnp.concatenate([proj_weight, jnp.zeros_like(proj_weight)], axis=0).reshape(
        2, own, -1
    )
    proj = jnp.transpose(proj, (2, 0, 1)).reshape(-1, 2 * own)
    params = jnp.concatenate([proj, *terms, jnp.zeros((1, 2 * own), BF16)], axis=0)
    params, _ = gather_seq([after(params, attended)] * (n_seq // 2), n_seq)
    channel_args = scan_arguments(dt_weight, dt_bias, a_log, skip_gain)
    in_columns = jnp.transpose(in_weight, (2, 1, 3, 0)).reshape(channels, features)
    far = after(far, in_columns)

    acc = call(
        functools.partial(own_kernel, n_seq),
        shape((seq_len, features), F32),
        n_seq + 2,
        [pltpu.VMEM((seq_len, width), BF16)],
        flops=2 * seq_len * features * width,
        size=seq_len * features * 8,
        limit=56,
    )(rank_arg, *own_pieces, out_weight, residual)
    far_pieces, others = gather_seq(
        [far] * (n_seq // 2),
        n_seq,
        acc, nearest, channel_args, *params,
    )
    acc, weights[1], channel_args, *params = others
    used = n_sec - 1
    payloads = call(
        functools.partial(mix_kernel, n_seq, used),
        [shape((HALO + rows, channels), BF16)] * n_seq,
        n_seq + used + 3,
        [
            pltpu.VMEM((seq_len, width * used), BF16),
            pltpu.VMEM((used * width, features), BF16),
            pltpu.VMEM((seq_len, features), F32),
            pltpu.VMEM((channels, features), BF16),
            pltpu.VMEM((seq_len, features), BF16),
            pltpu.VMEM((seq_len, channels), BF16),
            pltpu.VMEM((n_seq, HALO, channels), BF16),
            pltpu.VMEM((n_seq, rows), F32),
            pltpu.SemaphoreType.DMA((3 * n_seq + 2 * used + 3,)),
        ],
        flops=2 * seq_len * features * (width * used + channels),
        size=seq_len * features * 12,
        limit=56,
        in_place=[pl.ANY] * (n_seq + used + 1) + [pltpu.VMEM, pl.ANY],
        out_place=pl.ANY,
    )(
        rank_arg,
        *far_pieces,
        *[weights[r] for r in others_at],
        acc,
        norm_gain.reshape(1, -1),
        in_columns,
    )

    arrived = {k: swap(payloads[k], "seq", n_seq, 1) for k in range(n_seq - 1, 0, -2)}
    summed = {
        k: (payloads[k].astype(F32) + arrived[k + 1].astype(F32)).astype(BF16)
        for k in range(0, n_seq, 2)
    }
    pieces = [summed[0]] + [swap(summed[k], "seq", n_seq, k) for k in range(2, n_seq, 2)]

    map_rows = DT_RANK + 4 * NST
    outgoing, maps = call(
        functools.partial(conv_kernel, len(pieces), n_seq),
        [shape((n_seq, rows, 2 * own), BF16), shape((map_rows, rows), BF16)],
        len(pieces) + n_seq,
        [pltpu.VMEM((rows + 8, channels), F32)],
        flops=2 * rows * channels * map_rows,
        size=rows * channels * 12,
        limit=12 * scale,
    )(rank_arg, *pieces, *params)

    map_parts = [maps] + [swap(maps, "section", n_sec, r) for r in range(1, n_sec)]
    messages = call(
        functools.partial(sum_kernel, n_sec),
        [shape((2 * rows + map_rows, rows), BF16)] * (n_seq // 2),
        n_sec + 1,
        size=map_rows * rows * 2 * n_sec,
        limit=8 * scale,
    )(rank_arg, *map_parts, outgoing)
    scan_pieces, _ = gather_seq(messages, n_seq)

    wide = NST * own
    return call(
        functools.partial(scan_kernel, n_seq),
        shape((own, seq_len), BF16),
        n_seq + 4,
        [pltpu.VMEM((NST // 2, n_seq * (rows + PAD), 2 * own), F32)] * 2
        + [pltpu.VMEM((seq_len, wide), F32)]
        + [pltpu.VMEM((seq_len, 2 * own), F32)]
        + [pltpu.VMEM((n_seq, wide), F32)] * 3,
        flops=2 * seq_len * DT_RANK * own,
        size=seq_len * wide * 8,
        limit=16 * scale,
    )(rank_arg, *scan_pieces, *channel_args)


def solution(mesh):
    return jax.shard_map(
        functools.partial(body, mesh.shape["seq"], mesh.shape["section"]),
        mesh=mesh,
        in_specs=(
            P("seq", "section"),
            P("seq", "section"),
            P("seq", "section"),
            P(None, "seq"),
            P("section", "seq"),
            P("seq"),
            P("seq", None, None, "section"),
            P(("seq", "section"), None),
            P(("seq", "section")),
            P(("seq", "section"), None),
            P(None, ("seq", "section")),
            P(("seq", "section")),
            P(("seq", "section"), None),
            P(("seq", "section")),
        ),
        out_specs=P(("seq", "section"), None),
        check_vma=False,
    )
```

```python
import functools
import math

import jax
import jax.numpy as jnp
from jax import lax
from jax.experimental import pallas as pl
from jax.experimental.pallas import tpu as pltpu
from jax.sharding import PartitionSpec as P

D = 8192
HD = 128
GROUP = 4
NST = 8
DT_RANK = 256
CONV = 4
NORM_EPS = 1e-05
HALO = 16
PAD = 8
MIB = 1024 * 1024
VMEM_LIMIT = 56 * MIB

F32 = jnp.float32
BF16 = jnp.bfloat16

NN = (((1,), (0,)), ((), ()))
NT = (((1,), (1,)), ((), ()))
TN = (((0,), (0,)), ((), ()))


def dot(lhs, rhs, dims=NN):
    return lax.dot_general(lhs, rhs, dims, preferred_element_type=F32)


def call(kernel, out_shape, n_in, scratch=(), flops=0, size=0, in_place=None, out_place=pltpu.VMEM, limit=16):
    in_place = in_place or [pltpu.VMEM] * n_in
    return pl.pallas_call(
        kernel,
        out_shape=out_shape,
        in_specs=[pl.BlockSpec(memory_space=place) for place in [pltpu.SMEM] + in_place],
        out_specs=jax.tree.map(lambda _: pl.BlockSpec(memory_space=out_place), out_shape),
        scratch_shapes=list(scratch),
        compiler_params=pltpu.CompilerParams(vmem_limit_bytes=min(limit * MIB, VMEM_LIMIT)),
        cost_estimate=pl.CostEstimate(flops=flops, bytes_accessed=size, transcendentals=0),
    )


def swap(x, axis, count, bits):
    return lax.ppermute(x, axis, [(i, i ^ bits) for i in range(count)])


def after(x, *others):
    return lax.optimization_barrier((x, *others))[0]


def gather_seq(messages, count, *others):
    even = [messages[0]] + [swap(messages[k // 2], "seq", count, k) for k in range(2, count, 2)]
    even, others = lax.optimization_barrier((even, others))
    pieces = []
    for piece in even:
        pieces += [piece, swap(piece, "seq", count, 1)]
    return pieces, others


def attention_kernel(count, rank_ref, query_ref, *refs):
    kv_refs = refs[:count]
    out_ref, scores_ref, value_ref = refs[count:]
    rank = rank_ref[0]
    rows = query_ref.shape[0]
    stacked = jnp.concatenate(
        [query_ref[:, g * HD : (g + 1) * HD] for g in range(GROUP)], axis=0
    )
    maxima = None
    for k in range(count):
        part = dot(stacked, kv_refs[k][:, :HD], NT) * (1.0 / math.sqrt(HD))
        if k == 0:
            row = lax.broadcasted_iota(jnp.int32, part.shape, 0) % rows
            col = lax.broadcasted_iota(jnp.int32, part.shape, 1)
            part = jnp.where(row >= col, part, -1e30)
        else:
            earlier = jnp.bitwise_xor(rank, k) < rank
            part = jnp.where(earlier, part, -1e30)
        scores_ref[:, k * rows : (k + 1) * rows] = part
        value_ref[k * rows : (k + 1) * rows, :] = kv_refs[k][:, HD:]
        peak = jnp.max(part, axis=1, keepdims=True)
        maxima = peak if maxima is None else jnp.maximum(maxima, peak)
    terms = jnp.exp(scores_ref[...] - maxima)
    total = jnp.sum(terms, axis=1, keepdims=True)
    result = dot(terms.astype(BF16), value_ref[...]) / total
    result = result.astype(BF16)
    for g in range(GROUP):
        out_ref[:, g * HD : (g + 1) * HD] = result[g * rows : (g + 1) * rows, :]


def partner_sums(blocks, count):
    arrived = [swap(blocks[k + 1], "seq", count, 1) for k in range(0, count, 2)]
    return [
        (blocks[k].astype(F32) + arrived[k // 2].astype(F32)).astype(BF16)
        for k in range(0, count, 2)
    ]


def owner_pieces(sums, count):
    return [sums[0]] + [swap(sums[k // 2], "seq", count, k) for k in range(2, count, 2)]


class Copies:
    def __init__(self, semaphores):
        self.semaphores = semaphores
        self.count = 0

    def start(self, source, target):
        copy = pltpu.make_async_copy(source, target, self.semaphores.at[self.count])
        self.count += 1
        copy.start()
        return copy


def own_kernel(count, rank_ref, *refs):
    own_refs = refs[:count]
    weight_ref, residual_ref, acc_ref, left_ref = refs[count:]
    rank = rank_ref[0]
    rows = own_refs[0].shape[0]
    for k in range(count):
        left_ref[k * rows : (k + 1) * rows, :] = own_refs[k][...]
    tile = 2 * rows
    for t in range(count // 2):
        total = dot(left_ref[t * tile : (t + 1) * tile, :], weight_ref[...])
        for half in range(2):
            k = 2 * t + half
            first = pl.multiple_of(jnp.bitwise_xor(rank, k) * rows, rows)
            acc_ref[k * rows : (k + 1) * rows, :] = total[
                half * rows : (half + 1) * rows
            ] + residual_ref[pl.ds(first, rows), :].astype(F32)


def mix_kernel(count, used, rank_ref, *refs):
    far_refs = refs[:count]
    weight_refs = refs[count : count + used]
    refs = refs[count + used :]
    acc_ref, gain_ref, in_ref = refs[:3]
    path_refs, gate_refs = refs[3 : count + 3], refs[count + 3 : 2 * count + 3]
    left, weights, normed, mixed, halos, squares, semaphores = refs[2 * count + 3 :]
    rank = rank_ref[0]
    rows = far_refs[0].shape[0]
    width = weight_refs[0].shape[0]
    channels = in_ref.shape[0] // 2
    copies = Copies(semaphores)
    weight_copies = [
        copies.start(weight_refs[r], weights.at[pl.ds(r * width, width), :]) for r in range(used)
    ]
    tile = rows * count // 2
    left_copies, out_copies = [], []
    for t in range(2):
        left_copies.append(
            [
                copies.start(
                    far_refs[k],
                    left.at[pl.ds(k * rows, rows), :],
                )
                for k in range(t * count // 2, (t + 1) * count // 2)
            ]
        )
    for copy in weight_copies:
        copy.wait()
    eye = lax.broadcasted_iota(jnp.int32, (rows, rows), 0) == lax.broadcasted_iota(
        jnp.int32, (rows, rows), 1
    )
    for t in range(2):
        span = pl.ds(t * tile, tile)
        for copy in left_copies[t]:
            copy.wait()
        total = dot(left[span, :], weights[...])
        hidden = acc_ref[span, :] + total
        normed[span, :] = (hidden * gain_ref[...]).astype(BF16)
        sums = jnp.sum(hidden * hidden, axis=1, keepdims=True)
        for part in range(count // 2):
            k = t * count // 2 + part
            squares[k : k + 1, :] = jnp.sum(
                jnp.where(eye, sums[part * rows : (part + 1) * rows], 0.0),
                axis=0,
                keepdims=True,
            )
    for t in range(2):
        result = dot(normed[pl.ds(t * tile, tile), :], in_ref[...], NT).astype(BF16)
        mixed[pl.ds(t * tile, tile), :] = result
        for part in range(count // 2):
            k = t * count // 2 + part
            block = mixed.at[pl.ds(k * rows, rows), :]
            target = path_refs[k].at[pl.ds(HALO, rows), :]
            out_copies.append(copies.start(block.at[:, pl.ds(0, channels)], target))
            out_copies.append(copies.start(block.at[:, pl.ds(channels, channels)], gate_refs[k]))
    line = lax.broadcasted_iota(jnp.int32, (HALO, channels), 0)
    for k in range(count):
        block = jnp.bitwise_xor(rank, k)
        before = jnp.bitwise_xor(rank, jnp.maximum(block - 1, 0))
        last = pl.multiple_of(before * rows + (rows - HALO), HALO)
        halo = mixed[pl.ds(last, HALO), :channels].astype(F32)
        own = jnp.tile(squares[k : k + 1, :], (1, channels // rows))
        past = jnp.tile(squares[pl.ds(before, 1), :], (1, channels // rows))
        halo = jnp.where(line == 0, own, jnp.where(line == 1, past, halo))
        halos[k] = halo.astype(BF16)
        out_copies.append(copies.start(halos.at[k], path_refs[k].at[pl.ds(0, HALO), :]))
    for copy in out_copies:
        copy.wait()


def conv_kernel(n_pieces, count, rank_ref, *refs):
    piece_refs = refs[:n_pieces]
    param_refs = refs[n_pieces : n_pieces + count]
    out_ref, maps_ref, scale_ref, total_ref = refs[n_pieces + count :]
    rank = rank_ref[0]
    total = piece_refs[0][...].astype(F32)
    for piece in piece_refs[1:]:
        total += piece[...].astype(F32)
    rows = total.shape[0] - HALO
    eye = lax.broadcasted_iota(jnp.int32, (rows, rows), 0) == lax.broadcasted_iota(
        jnp.int32, (rows, rows), 1
    )
    scale_own = lax.rsqrt(total[0:1, :rows] / D + NORM_EPS)
    scale_past = lax.rsqrt(total[1:2, :rows] / D + NORM_EPS)
    scale_past = jnp.where(rank == 0, 0.0, scale_past)
    column_own = jnp.sum(jnp.where(eye, scale_own, 0.0), axis=1, keepdims=True)
    column_past = jnp.sum(jnp.where(eye, scale_past, 0.0), axis=1, keepdims=True)
    scale_ref[...] = column_own + jnp.zeros(scale_ref.shape, F32)
    total_ref[0:8, :] = total[HALO - 8 : HALO] * column_past[rows - 8 :]
    total_ref[8:, :] = total[HALO:] * column_own
    param_rows, group = param_refs[0].shape
    middle = DT_RANK + 2 * NST
    lane = lax.broadcasted_iota(jnp.int32, (param_rows, group), 1)
    parity = lane // (group // 2) == rank % 2
    projected = jnp.zeros((middle, rows), F32)
    for m in range(count // 2):
        first = pl.multiple_of(jnp.bitwise_xor(rank, 2 * m) // 2 * group, group)
        path = total_ref[:, pl.ds(first, group)]
        params = jnp.where(
            parity, param_refs[2 * m][...].astype(F32), param_refs[2 * m + 1][...].astype(F32)
        )
        taps = params[middle : middle + 5] + params[middle + 5 : middle + 10]
        taps += params[middle + 10 : middle + 15]
        conv = taps[CONV : CONV + 1] + jnp.zeros((rows, group), F32)
        for offset in range(CONV):
            begin = 8 - (CONV - 1) + offset
            conv += taps[offset : offset + 1] * path[begin : begin + rows]
        result = (conv / (1.0 + jnp.exp(-conv))).astype(BF16)
        out_ref[:, pl.ds(first, group)] = result
        projected += dot(params[0:middle].astype(BF16), result, NT)
    low_rank = projected[:DT_RANK]
    maps = projected[DT_RANK:]
    high = maps.astype(BF16)
    maps_ref[0:DT_RANK, :] = low_rank.astype(BF16)
    maps_ref[DT_RANK:middle, :] = high
    maps_ref[middle:, :] = (maps - high.astype(F32)).astype(BF16)


def sum_kernel(n_maps, n_gates, count, rank_ref, *refs):
    map_refs = refs[:n_maps]
    gate_refs = refs[n_maps : n_maps + n_gates]
    refs = refs[n_maps + n_gates :]
    inputs_ref, scale_ref = refs[:2]
    out_refs = refs[2 : 2 + count // 2]
    gate_scratch = refs[2 + count // 2]
    rank = rank_ref[0]
    total = map_refs[0][...].astype(F32)
    for piece in map_refs[1:]:
        total += piece[...].astype(F32)
    middle = DT_RANK + 2 * NST
    maps = total[DT_RANK:middle] + total[middle:]
    high = maps.astype(BF16)
    low = (maps - high.astype(F32)).astype(BF16)
    low_rank = total[:DT_RANK].astype(BF16)
    gate = gate_refs[0][...].astype(F32)
    for piece in gate_refs[1:]:
        gate += piece[...].astype(F32)
    gate = gate * scale_ref[:, 0:1]
    gate_scratch[...] = gate / (1.0 + jnp.exp(-gate))
    rows, group = scale_ref.shape
    lane = lax.broadcasted_iota(jnp.int32, (rows, group), 1)
    for at, out_ref in enumerate(out_refs):
        first = pl.multiple_of(jnp.bitwise_xor(rank, 2 * at) // 2 * group, group)
        inputs = inputs_ref[:, pl.ds(first, group)].astype(F32)
        gate = gate_scratch[:, pl.ds(first, group)]
        even = jnp.where(lane < group // 2, inputs, pltpu.roll(gate, group // 2, 1))
        odd = jnp.where(lane < group // 2, pltpu.roll(inputs, group // 2, 1), gate)
        out_ref[0:rows, :] = jnp.where(rank % 2 == 0, even, odd).astype(BF16)
        out_ref[rows : 2 * rows, :] = jnp.where(rank % 2 == 0, odd, even).astype(BF16)
        out_ref[2 * rows : 2 * rows + DT_RANK, :] = low_rank
        out_ref[2 * rows + DT_RANK : 2 * rows + middle, :] = high
        out_ref[2 * rows + middle :, :] = low


def scan_kernel(count, rank_ref, *refs):
    rows = (refs[0].shape[0] - DT_RANK - 4 * NST) // 2
    pair_refs = [refs[k].at[pl.ds(k % 2 * rows, rows), :] for k in range(count)]
    maps_refs = [refs[k].at[pl.ds(2 * rows, DT_RANK + 4 * NST), :] for k in range(count)]
    (
        weight_ref, bias_ref, decay_ref, skip_ref, out_ref,
        factor_ref, source_ref, read_ref, value_ref, end_ref, product_ref, begin_ref,
    ) = refs[count:]
    rank = rank_ref[0]
    pitch = rows + PAD
    lanes = weight_ref.shape[1]
    half = lanes // 2
    groups = NST // 2
    wide = groups * lanes
    map_rows = maps_refs[0].shape[0] - DT_RANK
    map_row = lax.broadcasted_iota(jnp.int32, (map_rows, wide), 0) % (2 * NST)
    state_of = lax.broadcasted_iota(jnp.int32, (map_rows, wide), 1) // half
    spread_in = jnp.where(map_row == state_of, 1.0, 0.0).astype(BF16)
    spread_out = jnp.where(map_row == state_of + NST, 1.0, 0.0).astype(BF16)
    lane = lax.broadcasted_iota(jnp.int32, (rows, lanes), 1)
    for k in range(count):
        span = slice(k * rows, (k + 1) * rows)
        padded = slice(k * pitch, k * pitch + rows)
        step = dot(maps_refs[k][:DT_RANK, :], weight_ref[...], TN) + bias_ref[...]
        step = jnp.maximum(step, 0.0) + jnp.log1p(jnp.exp(-jnp.abs(step)))
        pair = pair_refs[k][...].astype(F32)
        value = jnp.where(lane < half, pair, pltpu.roll(pair, half, 1))
        value_ref[span, :] = value
        maps = maps_refs[k][DT_RANK:, :]
        in_map = dot(maps, spread_in, TN)
        read_ref[span, :] = dot(maps, spread_out, TN)
        drive = step * value
        for g in range(groups):
            part = slice(g * lanes, (g + 1) * lanes)
            factor_ref[g, padded, :] = jnp.exp(step * decay_ref[:, part])
            source_ref[g, padded, :] = drive * in_map[:, part]

    def advance(t, carried):
        at = pl.ds(t, count, stride=pitch)
        following = []
        for g in range(groups):
            state, product = carried[g]
            factor = factor_ref[g, at, :]
            state = factor * state + source_ref[g, at, :]
            product = factor * product
            source_ref[g, at, :] = state
            factor_ref[g, at, :] = product
            following.append((state, product))
        return following

    carried = lax.fori_loop(
        0,
        rows,
        advance,
        [(jnp.zeros((count, lanes), F32), jnp.ones((count, lanes), F32))] * groups,
        unroll=8,
    )
    state = jnp.concatenate([pair[0] for pair in carried], axis=1)
    product = jnp.concatenate([pair[1] for pair in carried], axis=1)
    end_ref[...] = state
    product_ref[...] = product
    carried = jnp.zeros((1, wide), F32)
    for j in range(count):
        at = pl.ds(jnp.bitwise_xor(rank, j), 1)
        begin_ref[at, :] = carried
        carried = product_ref[at, :] * carried + end_ref[at, :]
    for k in range(count):
        span = slice(k * rows, (k + 1) * rows)
        padded = slice(k * pitch, k * pitch + rows)
        total = skip_ref[...] * value_ref[span, :]
        readout = jnp.zeros((rows, lanes), F32)
        for g in range(groups):
            part = slice(g * lanes, (g + 1) * lanes)
            state = source_ref[g, padded, :] + factor_ref[g, padded, :] * begin_ref[k : k + 1, part]
            readout += state * read_ref[span, part]
        total += readout + pltpu.roll(readout, half, 1)
        result = jnp.transpose(total * pair_refs[k][...].astype(F32))
        first = pl.multiple_of(jnp.bitwise_xor(rank, k) * rows, rows)
        out_ref[:, pl.ds(first, rows)] = result[half:].astype(BF16)


def scan_arguments(dt_weight, dt_bias, a_log, skip_gain):
    weight = jnp.concatenate([dt_weight, dt_weight], axis=1)
    bias = jnp.concatenate([dt_bias, dt_bias]).reshape(1, -1)
    skip = jnp.concatenate([skip_gain, skip_gain]).reshape(1, -1)
    decay = (-jnp.exp(a_log)).T.reshape(1, -1)
    return weight, bias, decay, skip


def body(
    n_seq,
    n_sec,
    queries,
    keys,
    values,
    residual,
    out_weight,
    norm_gain,
    in_weight,
    conv_weight,
    conv_bias,
    proj_weight,
    dt_weight,
    dt_bias,
    a_log,
    skip_gain,
):
    shape = jax.ShapeDtypeStruct
    rows = queries.shape[0]
    seq_len = residual.shape[0]
    features = residual.shape[1]
    scale = -(-seq_len // 1024)
    own = conv_weight.shape[0]
    channels = n_seq * 2 * own
    rank = lax.axis_index("seq").astype(jnp.int32)
    rank_arg = rank.reshape(1)

    others_at = list(range(1, n_sec))
    far_at = list(range(3, n_sec, 2))
    weights = {r: swap(out_weight, "section", n_sec, r) for r in far_at}

    pairs, _ = gather_seq([jnp.concatenate([keys, values], axis=1)] * (n_seq // 2), n_seq)
    attended = call(
        functools.partial(attention_kernel, n_seq),
        shape((rows, GROUP * HD), BF16),
        1 + n_seq,
        [pltpu.VMEM((GROUP * rows, seq_len), F32), pltpu.VMEM((seq_len, HD), BF16)],
        flops=4 * GROUP * rows * seq_len * HD,
        size=4 * rows * 4 * HD * n_seq,
        limit=16 * scale,
    )(rank_arg, queries, *pairs)

    far = jnp.concatenate(
        [swap(attended, "section", n_sec, r) for r in others_at], axis=1
    )
    own_pieces, _ = gather_seq([attended] * (n_seq // 2), n_seq)
    nearest = swap(after(out_weight, own_pieces[-1]), "section", n_sec, 1)
    for r in range(2, n_sec, 2):
        weights[r] = swap(after(weights[r + 1], far), "section", n_sec, 1)

    width = out_weight.shape[0]
    conv = jnp.concatenate([conv_weight, conv_bias[:, None]], axis=1).T
    terms = [proj_weight.T]
    for _ in range(3):
        high = lax.reduce_precision(conv, 8, 7)
        terms.append(high.astype(BF16))
        conv = conv - high
    params = jnp.concatenate([*terms, jnp.zeros((1, own), BF16)], axis=0)
    params = jnp.concatenate([params, params], axis=1)
    params, _ = gather_seq([after(params, attended)] * (n_seq // 2), n_seq)
    channel_args = scan_arguments(dt_weight, dt_bias, a_log, skip_gain)
    in_columns = jnp.transpose(in_weight, (1, 2, 3, 0)).reshape(channels, features)
    far = after(far, in_columns)

    acc = call(
        functools.partial(own_kernel, n_seq),
        shape((seq_len, features), F32),
        n_seq + 2,
        [pltpu.VMEM((seq_len, width), BF16)],
        flops=2 * seq_len * features * width,
        size=seq_len * features * 8,
        limit=56,
    )(rank_arg, *own_pieces, out_weight, residual)
    far_pieces, others = gather_seq(
        [far] * (n_seq // 2),
        n_seq,
        acc, nearest, channel_args, *params,
    )
    acc, weights[1], channel_args, *params = others
    used = n_sec - 1
    payloads = call(
        functools.partial(mix_kernel, n_seq, used),
        [shape((HALO + rows, channels // 2), BF16)] * n_seq
        + [shape((rows, channels // 2), BF16)] * n_seq,
        n_seq + used + 3,
        [
            pltpu.VMEM((seq_len, width * used), BF16),
            pltpu.VMEM((used * width, features), BF16),
            pltpu.VMEM((seq_len, features), BF16),
            pltpu.VMEM((seq_len, channels), BF16),
            pltpu.VMEM((n_seq, HALO, channels // 2), BF16),
            pltpu.VMEM((n_seq, rows), F32),
            pltpu.SemaphoreType.DMA((4 * n_seq + used,)),
        ],
        flops=2 * seq_len * features * (width * used + channels),
        size=seq_len * features * 12,
        limit=28 * scale,
        in_place=[pl.ANY] * (n_seq + used) + [pltpu.VMEM] * 3,
        out_place=pl.ANY,
    )(
        rank_arg,
        *far_pieces,
        *[weights[r] for r in others_at],
        acc,
        norm_gain.reshape(1, -1),
        in_columns,
    )

    path_sums = partner_sums(payloads[:n_seq], n_seq)
    path_pieces = owner_pieces(path_sums, n_seq)
    gates = [after(gate, *path_sums) for gate in payloads[n_seq:]]
    gate_pieces = owner_pieces(partner_sums(gates, n_seq), n_seq)

    map_rows = DT_RANK + 4 * NST
    inputs, maps, scales = call(
        functools.partial(conv_kernel, len(path_pieces), n_seq),
        [
            shape((rows, channels // 2), BF16),
            shape((map_rows, rows), BF16),
            shape((rows, 2 * own), F32),
        ],
        len(path_pieces) + n_seq,
        [pltpu.VMEM((rows + 8, channels // 2), F32)],
        flops=rows * channels * map_rows,
        size=rows * channels * 6,
        limit=12 * scale,
    )(rank_arg, *path_pieces, *params)

    map_parts = [maps] + [swap(maps, "section", n_sec, r) for r in range(1, n_sec)]
    messages = call(
        functools.partial(sum_kernel, n_sec, len(gate_pieces), n_seq),
        [shape((2 * rows + map_rows, rows), BF16)] * (n_seq // 2),
        n_sec + len(gate_pieces) + 2,
        [pltpu.VMEM((rows, channels // 2), F32)],
        size=map_rows * rows * 2 * n_sec,
        limit=8 * scale,
    )(rank_arg, *map_parts, *gate_pieces, inputs, scales)
    scan_pieces, _ = gather_seq(messages, n_seq)

    wide = NST * own
    return call(
        functools.partial(scan_kernel, n_seq),
        shape((own, seq_len), BF16),
        n_seq + 4,
        [pltpu.VMEM((NST // 2, n_seq * (rows + PAD), 2 * own), F32)] * 2
        + [pltpu.VMEM((seq_len, wide), F32)]
        + [pltpu.VMEM((seq_len, 2 * own), F32)]
        + [pltpu.VMEM((n_seq, wide), F32)] * 3,
        flops=2 * seq_len * DT_RANK * own,
        size=seq_len * wide * 8,
        limit=16 * scale,
    )(rank_arg, *scan_pieces, *channel_args)


def solution(mesh):
    return jax.shard_map(
        functools.partial(body, mesh.shape["seq"], mesh.shape["section"]),
        mesh=mesh,
        in_specs=(
            P("seq", "section"),
            P("seq", "section"),
            P("seq", "section"),
            P(None, "seq"),
            P("section", "seq"),
            P("seq"),
            P("seq", None, None, "section"),
            P(("seq", "section"), None),
            P(("seq", "section")),
            P(("seq", "section"), None),
            P(None, ("seq", "section")),
            P(("seq", "section")),
            P(("seq", "section"), None),
            P(("seq", "section")),
        ),
        out_specs=P(("seq", "section"), None),
        check_vma=False,
    )
```

```python
import functools
import math

import jax
import jax.numpy as jnp
from jax import lax
from jax.experimental import pallas as pl
from jax.experimental.pallas import tpu as pltpu
from jax.sharding import PartitionSpec as P

D = 8192
HD = 128
GROUP = 4
NST = 8
DT_RANK = 256
CONV = 4
NORM_EPS = 1e-05
HALO = 16
PAD = 8
MIB = 1024 * 1024
VMEM_LIMIT = 56 * MIB

F32 = jnp.float32
BF16 = jnp.bfloat16

NN = (((1,), (0,)), ((), ()))
NT = (((1,), (1,)), ((), ()))
TN = (((0,), (0,)), ((), ()))


def dot(lhs, rhs, dims=NN):
    return lax.dot_general(lhs, rhs, dims, preferred_element_type=F32)


def call(kernel, out_shape, n_in, scratch=(), flops=0, size=0, in_place=None, out_place=pltpu.VMEM, limit=16):
    in_place = in_place or [pltpu.VMEM] * n_in
    return pl.pallas_call(
        kernel,
        out_shape=out_shape,
        in_specs=[pl.BlockSpec(memory_space=place) for place in [pltpu.SMEM] + in_place],
        out_specs=jax.tree.map(lambda _: pl.BlockSpec(memory_space=out_place), out_shape),
        scratch_shapes=list(scratch),
        compiler_params=pltpu.CompilerParams(vmem_limit_bytes=min(limit * MIB, VMEM_LIMIT)),
        cost_estimate=pl.CostEstimate(flops=flops, bytes_accessed=size, transcendentals=0),
    )


def swap(x, axis, count, bits):
    return lax.ppermute(x, axis, [(i, i ^ bits) for i in range(count)])


def after(x, *others):
    return lax.optimization_barrier((x, *others))[0]


def gather_seq(messages, count, *others):
    even = [messages[0]] + [swap(messages[k // 2], "seq", count, k) for k in range(2, count, 2)]
    even, others = lax.optimization_barrier((even, others))
    pieces = []
    for piece in even:
        pieces += [piece, swap(piece, "seq", count, 1)]
    return pieces, others


def attention_kernel(count, rank_ref, query_ref, *refs):
    kv_refs = refs[:count]
    out_ref, scores_ref, value_ref = refs[count:]
    rank = rank_ref[0]
    rows = query_ref.shape[0]
    stacked = jnp.concatenate(
        [query_ref[:, g * HD : (g + 1) * HD] for g in range(GROUP)], axis=0
    )
    maxima = None
    for k in range(count):
        part = dot(stacked, kv_refs[k][:, :HD], NT) * (1.0 / math.sqrt(HD))
        if k == 0:
            row = lax.broadcasted_iota(jnp.int32, part.shape, 0) % rows
            col = lax.broadcasted_iota(jnp.int32, part.shape, 1)
            part = jnp.where(row >= col, part, -1e30)
        else:
            earlier = jnp.bitwise_xor(rank, k) < rank
            part = jnp.where(earlier, part, -1e30)
        scores_ref[:, k * rows : (k + 1) * rows] = part
        value_ref[k * rows : (k + 1) * rows, :] = kv_refs[k][:, HD:]
        peak = jnp.max(part, axis=1, keepdims=True)
        maxima = peak if maxima is None else jnp.maximum(maxima, peak)
    terms = jnp.exp(scores_ref[...] - maxima)
    total = jnp.sum(terms, axis=1, keepdims=True)
    result = dot(terms.astype(BF16), value_ref[...]) / total
    result = result.astype(BF16)
    for g in range(GROUP):
        out_ref[:, g * HD : (g + 1) * HD] = result[g * rows : (g + 1) * rows, :]


def partner_sums(blocks, count):
    arrived = [swap(blocks[k + 1], "seq", count, 1) for k in range(0, count, 2)]
    return [
        (blocks[k].astype(F32) + arrived[k // 2].astype(F32)).astype(BF16)
        for k in range(0, count, 2)
    ]


def owner_pieces(sums, count):
    return [sums[0]] + [swap(sums[k // 2], "seq", count, k) for k in range(2, count, 2)]


class Copies:
    def __init__(self, semaphores):
        self.semaphores = semaphores
        self.count = 0

    def start(self, source, target):
        copy = pltpu.make_async_copy(source, target, self.semaphores.at[self.count])
        self.count += 1
        copy.start()
        return copy


def own_kernel(count, rank_ref, *refs):
    own_refs = refs[:count]
    weight_ref, residual_ref, acc_ref, left_ref = refs[count:]
    rank = rank_ref[0]
    rows = own_refs[0].shape[0]
    for k in range(count):
        left_ref[k * rows : (k + 1) * rows, :] = own_refs[k][...]
    tile = 2 * rows
    for t in range(count // 2):
        total = dot(left_ref[t * tile : (t + 1) * tile, :], weight_ref[...])
        for half in range(2):
            k = 2 * t + half
            first = pl.multiple_of(jnp.bitwise_xor(rank, k) * rows, rows)
            rest = residual_ref[pl.ds(first, rows), :].astype(F32)
            acc_ref[k * rows : (k + 1) * rows, :] = (
                total[half * rows : (half + 1) * rows] + rest
            ).astype(BF16)


def mix_kernel(count, used, rank_ref, *refs):
    far_refs = refs[:count]
    weight_refs = refs[count : count + used]
    refs = refs[count + used :]
    acc_ref, gain_ref, in_ref = refs[:3]
    path_refs, gate_refs = refs[3 : count + 3], refs[count + 3 : 2 * count + 3]
    left, weights, normed, mixed, halos, squares, semaphores = refs[2 * count + 3 :]
    rank = rank_ref[0]
    rows = far_refs[0].shape[0]
    width = weight_refs[0].shape[0]
    channels = in_ref.shape[0] // 2
    copies = Copies(semaphores)
    tile = rows * count // 2
    spans = [pl.ds(r * width, width) for r in range(used)]
    weight_copies = [copies.start(weight_refs[0], weights.at[spans[0], :])]
    left_copies, out_copies = [], []
    for t in range(2):
        left_copies.append(
            [
                copies.start(
                    far_refs[k],
                    left.at[pl.ds(k * rows, rows), :],
                )
                for k in range(t * count // 2, (t + 1) * count // 2)
            ]
        )
        if t == 0:
            for r in range(1, used):
                weight_copies.append(copies.start(weight_refs[r], weights.at[spans[r], :]))
    eye = lax.broadcasted_iota(jnp.int32, (rows, rows), 0) == lax.broadcasted_iota(
        jnp.int32, (rows, rows), 1
    )
    for t in range(2):
        span = pl.ds(t * tile, tile)
        for copy in left_copies[t]:
            copy.wait()
        hidden = acc_ref[span, :].astype(F32)
        for r in range(used):
            if t == 0:
                weight_copies[r].wait()
            hidden += dot(left[span, spans[r]], weights[spans[r], :])
        normed[span, :] = (hidden * gain_ref[...]).astype(BF16)
        sums = jnp.sum(hidden * hidden, axis=1, keepdims=True)
        for part in range(count // 2):
            k = t * count // 2 + part
            squares[k : k + 1, :] = jnp.sum(
                jnp.where(eye, sums[part * rows : (part + 1) * rows], 0.0),
                axis=0,
                keepdims=True,
            )
    for t in range(2):
        result = dot(normed[pl.ds(t * tile, tile), :], in_ref[...], NT).astype(BF16)
        mixed[pl.ds(t * tile, tile), :] = result
        for part in range(count // 2):
            k = t * count // 2 + part
            block = mixed.at[pl.ds(k * rows, rows), :]
            target = path_refs[k].at[pl.ds(HALO, rows), :]
            out_copies.append(copies.start(block.at[:, pl.ds(0, channels)], target))
            out_copies.append(copies.start(block.at[:, pl.ds(channels, channels)], gate_refs[k]))
    line = lax.broadcasted_iota(jnp.int32, (HALO, channels), 0)
    for k in range(count):
        block = jnp.bitwise_xor(rank, k)
        before = jnp.bitwise_xor(rank, jnp.maximum(block - 1, 0))
        last = pl.multiple_of(before * rows + (rows - HALO), HALO)
        halo = mixed[pl.ds(last, HALO), :channels].astype(F32)
        own = jnp.tile(squares[k : k + 1, :], (1, channels // rows))
        past = jnp.tile(squares[pl.ds(before, 1), :], (1, channels // rows))
        halo = jnp.where(line == 0, own, jnp.where(line == 1, past, halo))
        halos[k] = halo.astype(BF16)
        out_copies.append(copies.start(halos.at[k], path_refs[k].at[pl.ds(0, HALO), :]))
    for copy in out_copies:
        copy.wait()


def conv_kernel(n_pieces, count, rank_ref, *refs):
    piece_refs = refs[:n_pieces]
    param_refs = refs[n_pieces : n_pieces + count]
    out_ref, maps_ref, scale_ref, total_ref = refs[n_pieces + count :]
    rank = rank_ref[0]
    total = piece_refs[0][...].astype(F32)
    for piece in piece_refs[1:]:
        total += piece[...].astype(F32)
    rows = total.shape[0] - HALO
    eye = lax.broadcasted_iota(jnp.int32, (rows, rows), 0) == lax.broadcasted_iota(
        jnp.int32, (rows, rows), 1
    )
    scale_own = lax.rsqrt(total[0:1, :rows] / D + NORM_EPS)
    scale_past = lax.rsqrt(total[1:2, :rows] / D + NORM_EPS)
    scale_past = jnp.where(rank == 0, 0.0, scale_past)
    column_own = jnp.sum(jnp.where(eye, scale_own, 0.0), axis=1, keepdims=True)
    column_past = jnp.sum(jnp.where(eye, scale_past, 0.0), axis=1, keepdims=True)
    scale_ref[...] = column_own + jnp.zeros(scale_ref.shape, F32)
    total_ref[0:8, :] = total[HALO - 8 : HALO] * column_past[rows - 8 :]
    total_ref[8:, :] = total[HALO:] * column_own
    param_rows, group = param_refs[0].shape
    middle = DT_RANK + 2 * NST
    lane = lax.broadcasted_iota(jnp.int32, (param_rows, group), 1)
    parity = lane // (group // 2) == rank % 2
    projected = jnp.zeros((middle, rows), F32)
    for m in range(count // 2):
        first = pl.multiple_of(jnp.bitwise_xor(rank, 2 * m) // 2 * group, group)
        path = total_ref[:, pl.ds(first, group)]
        params = jnp.where(
            parity, param_refs[2 * m][...].astype(F32), param_refs[2 * m + 1][...].astype(F32)
        )
        taps = params[middle : middle + 5] + params[middle + 5 : middle + 10]
        taps += params[middle + 10 : middle + 15]
        conv = taps[CONV : CONV + 1] + jnp.zeros((rows, group), F32)
        for offset in range(CONV):
            begin = 8 - (CONV - 1) + offset
            conv += taps[offset : offset + 1] * path[begin : begin + rows]
        result = (conv / (1.0 + jnp.exp(-conv))).astype(BF16)
        out_ref[:, pl.ds(first, group)] = result
        projected += dot(params[0:middle].astype(BF16), result, NT)
    low_rank = projected[:DT_RANK]
    maps = projected[DT_RANK:]
    high = maps.astype(BF16)
    maps_ref[0:DT_RANK, :] = low_rank.astype(BF16)
    maps_ref[DT_RANK:middle, :] = high
    maps_ref[middle:, :] = (maps - high.astype(F32)).astype(BF16)


def sum_kernel(n_maps, n_gates, count, rank_ref, *refs):
    map_refs = refs[:n_maps]
    gate_refs = refs[n_maps : n_maps + n_gates]
    refs = refs[n_maps + n_gates :]
    inputs_ref, scale_ref = refs[:2]
    out_refs = refs[2 : 2 + count // 2]
    gate_scratch = refs[2 + count // 2]
    rank = rank_ref[0]
    total = map_refs[0][...].astype(F32)
    for piece in map_refs[1:]:
        total += piece[...].astype(F32)
    middle = DT_RANK + 2 * NST
    maps = total[DT_RANK:middle] + total[middle:]
    high = maps.astype(BF16)
    low = (maps - high.astype(F32)).astype(BF16)
    low_rank = total[:DT_RANK].astype(BF16)
    gate = gate_refs[0][...].astype(F32)
    for piece in gate_refs[1:]:
        gate += piece[...].astype(F32)
    gate = gate * scale_ref[:, 0:1]
    gate_scratch[...] = gate / (1.0 + jnp.exp(-gate))
    rows, group = scale_ref.shape
    lane = lax.broadcasted_iota(jnp.int32, (rows, group), 1)
    for at, out_ref in enumerate(out_refs):
        first = pl.multiple_of(jnp.bitwise_xor(rank, 2 * at) // 2 * group, group)
        inputs = inputs_ref[:, pl.ds(first, group)].astype(F32)
        gate = gate_scratch[:, pl.ds(first, group)]
        even = jnp.where(lane < group // 2, inputs, pltpu.roll(gate, group // 2, 1))
        odd = jnp.where(lane < group // 2, pltpu.roll(inputs, group // 2, 1), gate)
        out_ref[0:rows, :] = jnp.where(rank % 2 == 0, even, odd).astype(BF16)
        out_ref[rows : 2 * rows, :] = jnp.where(rank % 2 == 0, odd, even).astype(BF16)
        out_ref[2 * rows : 2 * rows + DT_RANK, :] = low_rank
        out_ref[2 * rows + DT_RANK : 2 * rows + middle, :] = high
        out_ref[2 * rows + middle :, :] = low


def scan_kernel(count, rank_ref, *refs):
    rows = (refs[0].shape[0] - DT_RANK - 4 * NST) // 2
    pair_refs = [refs[k].at[pl.ds(k % 2 * rows, rows), :] for k in range(count)]
    maps_refs = [refs[k].at[pl.ds(2 * rows, DT_RANK + 4 * NST), :] for k in range(count)]
    (
        weight_ref, bias_ref, decay_ref, skip_ref, out_ref,
        factor_ref, source_ref, read_ref, value_ref, end_ref, product_ref, begin_ref,
    ) = refs[count:]
    rank = rank_ref[0]
    pitch = rows + PAD
    lanes = weight_ref.shape[1]
    half = lanes // 2
    groups = NST // 2
    wide = groups * lanes
    map_rows = maps_refs[0].shape[0] - DT_RANK
    map_row = lax.broadcasted_iota(jnp.int32, (map_rows, wide), 0) % (2 * NST)
    state_of = lax.broadcasted_iota(jnp.int32, (map_rows, wide), 1) // half
    spread_in = jnp.where(map_row == state_of, 1.0, 0.0).astype(BF16)
    spread_out = jnp.where(map_row == state_of + NST, 1.0, 0.0).astype(BF16)
    lane = lax.broadcasted_iota(jnp.int32, (rows, lanes), 1)
    for k in range(count):
        span = slice(k * rows, (k + 1) * rows)
        padded = slice(k * pitch, k * pitch + rows)
        step = dot(maps_refs[k][:DT_RANK, :], weight_ref[...], TN) + bias_ref[...]
        step = jnp.maximum(step, 0.0) + jnp.log1p(jnp.exp(-jnp.abs(step)))
        pair = pair_refs[k][...].astype(F32)
        value = jnp.where(lane < half, pair, pltpu.roll(pair, half, 1))
        value_ref[span, :] = value
        maps = maps_refs[k][DT_RANK:, :]
        in_map = dot(maps, spread_in, TN)
        read_ref[span, :] = dot(maps, spread_out, TN)
        drive = step * value
        for g in range(groups):
            part = slice(g * lanes, (g + 1) * lanes)
            factor_ref[g, padded, :] = jnp.exp(step * decay_ref[:, part])
            source_ref[g, padded, :] = drive * in_map[:, part]

    def advance(t, carried):
        at = pl.ds(t, count, stride=pitch)
        following = []
        for g in range(groups):
            state, product = carried[g]
            factor = factor_ref[g, at, :]
            state = factor * state + source_ref[g, at, :]
            product = factor * product
            source_ref[g, at, :] = state
            factor_ref[g, at, :] = product
            following.append((state, product))
        return following

    carried = lax.fori_loop(
        0,
        rows,
        advance,
        [(jnp.zeros((count, lanes), F32), jnp.ones((count, lanes), F32))] * groups,
        unroll=8,
    )
    state = jnp.concatenate([pair[0] for pair in carried], axis=1)
    product = jnp.concatenate([pair[1] for pair in carried], axis=1)
    end_ref[...] = state
    product_ref[...] = product
    carried = jnp.zeros((1, wide), F32)
    for j in range(count):
        at = pl.ds(jnp.bitwise_xor(rank, j), 1)
        begin_ref[at, :] = carried
        carried = product_ref[at, :] * carried + end_ref[at, :]
    for k in range(count):
        span = slice(k * rows, (k + 1) * rows)
        padded = slice(k * pitch, k * pitch + rows)
        total = skip_ref[...] * value_ref[span, :]
        readout = jnp.zeros((rows, lanes), F32)
        for g in range(groups):
            part = slice(g * lanes, (g + 1) * lanes)
            state = source_ref[g, padded, :] + factor_ref[g, padded, :] * begin_ref[k : k + 1, part]
            readout += state * read_ref[span, part]
        total += readout + pltpu.roll(readout, half, 1)
        result = jnp.transpose(total * pair_refs[k][...].astype(F32))
        first = pl.multiple_of(jnp.bitwise_xor(rank, k) * rows, rows)
        out_ref[:, pl.ds(first, rows)] = result[half:].astype(BF16)


def scan_arguments(dt_weight, dt_bias, a_log, skip_gain):
    weight = jnp.concatenate([dt_weight, dt_weight], axis=1)
    bias = jnp.concatenate([dt_bias, dt_bias]).reshape(1, -1)
    skip = jnp.concatenate([skip_gain, skip_gain]).reshape(1, -1)
    decay = (-jnp.exp(a_log)).T.reshape(1, -1)
    return weight, bias, decay, skip


def body(
    n_seq,
    n_sec,
    queries,
    keys,
    values,
    residual,
    out_weight,
    norm_gain,
    in_weight,
    conv_weight,
    conv_bias,
    proj_weight,
    dt_weight,
    dt_bias,
    a_log,
    skip_gain,
):
    shape = jax.ShapeDtypeStruct
    rows = queries.shape[0]
    seq_len = residual.shape[0]
    features = residual.shape[1]
    scale = -(-seq_len // 1024)
    own = conv_weight.shape[0]
    channels = n_seq * 2 * own
    rank = lax.axis_index("seq").astype(jnp.int32)
    rank_arg = rank.reshape(1)

    others_at = list(range(1, n_sec))
    far_at = list(range(3, n_sec, 2))
    weights = {r: swap(out_weight, "section", n_sec, r) for r in far_at}
    nearest = swap(out_weight, "section", n_sec, 1)

    pairs, _ = gather_seq([jnp.concatenate([keys, values], axis=1)] * (n_seq // 2), n_seq)
    attended = call(
        functools.partial(attention_kernel, n_seq),
        shape((rows, GROUP * HD), BF16),
        1 + n_seq,
        [pltpu.VMEM((GROUP * rows, seq_len), F32), pltpu.VMEM((seq_len, HD), BF16)],
        flops=4 * GROUP * rows * seq_len * HD,
        size=4 * rows * 4 * HD * n_seq,
        limit=16 * scale,
    )(rank_arg, queries, *pairs)

    far = jnp.concatenate(
        [swap(attended, "section", n_sec, r) for r in others_at], axis=1
    )
    own_pieces, _ = gather_seq([attended] * (n_seq // 2), n_seq)
    far = after(far, nearest)
    for r in range(2, n_sec, 2):
        weights[r] = swap(after(weights[r + 1], far), "section", n_sec, 1)

    width = out_weight.shape[0]
    conv = jnp.concatenate([conv_weight, conv_bias[:, None]], axis=1).T
    terms = [proj_weight.T]
    for _ in range(3):
        high = lax.reduce_precision(conv, 8, 7)
        terms.append(high.astype(BF16))
        conv = conv - high
    params = jnp.concatenate([*terms, jnp.zeros((1, own), BF16)], axis=0)
    params = jnp.concatenate([params, params], axis=1)
    params, _ = gather_seq([after(params, attended)] * (n_seq // 2), n_seq)
    channel_args = scan_arguments(dt_weight, dt_bias, a_log, skip_gain)
    in_columns = jnp.transpose(in_weight, (1, 2, 3, 0)).reshape(channels, features)
    far = after(far, in_columns)

    acc = call(
        functools.partial(own_kernel, n_seq),
        shape((seq_len, features), BF16),
        n_seq + 2,
        [pltpu.VMEM((seq_len, width), BF16)],
        flops=2 * seq_len * features * width,
        size=seq_len * features * 8,
        limit=56,
    )(rank_arg, *own_pieces, out_weight, residual)
    far_pieces, others = gather_seq(
        [far] * (n_seq // 2),
        n_seq,
        acc, nearest, channel_args, *params,
    )
    acc, weights[1], channel_args, *params = others
    used = n_sec - 1
    payloads = call(
        functools.partial(mix_kernel, n_seq, used),
        [shape((HALO + rows, channels // 2), BF16)] * n_seq
        + [shape((rows, channels // 2), BF16)] * n_seq,
        n_seq + used + 3,
        [
            pltpu.VMEM((seq_len, width * used), BF16),
            pltpu.VMEM((used * width, features), BF16),
            pltpu.VMEM((seq_len, features), BF16),
            pltpu.VMEM((seq_len, channels), BF16),
            pltpu.VMEM((n_seq, HALO, channels // 2), BF16),
            pltpu.VMEM((n_seq, rows), F32),
            pltpu.SemaphoreType.DMA((4 * n_seq + used,)),
        ],
        flops=2 * seq_len * features * (width * used + channels),
        size=seq_len * features * 12,
        limit=28 * scale,
        in_place=[pl.ANY] * (n_seq + used) + [pltpu.VMEM] * 3,
        out_place=pl.ANY,
    )(
        rank_arg,
        *far_pieces,
        *[weights[r] for r in others_at],
        acc,
        norm_gain.reshape(1, -1),
        in_columns,
    )

    path_sums = partner_sums(payloads[:n_seq], n_seq)
    path_pieces = owner_pieces(path_sums, n_seq)
    gates = [after(gate, *path_sums) for gate in payloads[n_seq:]]
    gate_pieces = owner_pieces(partner_sums(gates, n_seq), n_seq)

    map_rows = DT_RANK + 4 * NST
    inputs, maps, scales = call(
        functools.partial(conv_kernel, len(path_pieces), n_seq),
        [
            shape((rows, channels // 2), BF16),
            shape((map_rows, rows), BF16),
            shape((rows, 2 * own), F32),
        ],
        len(path_pieces) + n_seq,
        [pltpu.VMEM((rows + 8, channels // 2), F32)],
        flops=rows * channels * map_rows,
        size=rows * channels * 6,
        limit=12 * scale,
    )(rank_arg, *path_pieces, *params)

    map_parts = [maps] + [swap(maps, "section", n_sec, r) for r in range(1, n_sec)]
    messages = call(
        functools.partial(sum_kernel, n_sec, len(gate_pieces), n_seq),
        [shape((2 * rows + map_rows, rows), BF16)] * (n_seq // 2),
        n_sec + len(gate_pieces) + 2,
        [pltpu.VMEM((rows, channels // 2), F32)],
        size=map_rows * rows * 2 * n_sec,
        limit=8 * scale,
    )(rank_arg, *map_parts, *gate_pieces, inputs, scales)
    scan_pieces, _ = gather_seq(messages, n_seq)

    wide = NST * own
    return call(
        functools.partial(scan_kernel, n_seq),
        shape((own, seq_len), BF16),
        n_seq + 4,
        [pltpu.VMEM((NST // 2, n_seq * (rows + PAD), 2 * own), F32)] * 2
        + [pltpu.VMEM((seq_len, wide), F32)]
        + [pltpu.VMEM((seq_len, 2 * own), F32)]
        + [pltpu.VMEM((n_seq, wide), F32)] * 3,
        flops=2 * seq_len * DT_RANK * own,
        size=seq_len * wide * 8,
        limit=16 * scale,
    )(rank_arg, *scan_pieces, *channel_args)


def solution(mesh):
    return jax.shard_map(
        functools.partial(body, mesh.shape["seq"], mesh.shape["section"]),
        mesh=mesh,
        in_specs=(
            P("seq", "section"),
            P("seq", "section"),
            P("seq", "section"),
            P(None, "seq"),
            P("section", "seq"),
            P("seq"),
            P("seq", None, None, "section"),
            P(("seq", "section"), None),
            P(("seq", "section")),
            P(("seq", "section"), None),
            P(None, ("seq", "section")),
            P(("seq", "section")),
            P(("seq", "section"), None),
            P(("seq", "section")),
        ),
        out_specs=P(("seq", "section"), None),
        check_vma=False,
    )
```

```python
import functools
import math

import jax
import jax.numpy as jnp
from jax import lax
from jax.experimental import pallas as pl
from jax.experimental.pallas import tpu as pltpu
from jax.sharding import PartitionSpec as P

D = 8192
HD = 128
GROUP = 4
NST = 8
DT_RANK = 256
CONV = 4
NORM_EPS = 1e-05
HALO = 16
PAD = 8
MIB = 1024 * 1024
VMEM_LIMIT = 56 * MIB

F32 = jnp.float32
BF16 = jnp.bfloat16

NN = (((1,), (0,)), ((), ()))
NT = (((1,), (1,)), ((), ()))
TN = (((0,), (0,)), ((), ()))


def dot(lhs, rhs, dims=NN):
    return lax.dot_general(lhs, rhs, dims, preferred_element_type=F32)


def call(kernel, out_shape, n_in, scratch=(), flops=0, size=0, in_place=None, out_place=pltpu.VMEM, limit=16):
    in_place = in_place or [pltpu.VMEM] * n_in
    return pl.pallas_call(
        kernel,
        out_shape=out_shape,
        in_specs=[pl.BlockSpec(memory_space=place) for place in [pltpu.SMEM] + in_place],
        out_specs=jax.tree.map(lambda _: pl.BlockSpec(memory_space=out_place), out_shape),
        scratch_shapes=list(scratch),
        compiler_params=pltpu.CompilerParams(vmem_limit_bytes=min(limit * MIB, VMEM_LIMIT)),
        cost_estimate=pl.CostEstimate(flops=flops, bytes_accessed=size, transcendentals=0),
    )


def swap(x, axis, count, bits):
    return lax.ppermute(x, axis, [(i, i ^ bits) for i in range(count)])


def after(x, *others):
    return lax.optimization_barrier((x, *others))[0]


def gather_seq(messages, count, *others):
    even = [messages[0]] + [swap(messages[k // 2], "seq", count, k) for k in range(2, count, 2)]
    even, others = lax.optimization_barrier((even, others))
    pieces = []
    for piece in even:
        pieces += [piece, swap(piece, "seq", count, 1)]
    return pieces, others


def attention_kernel(count, rank_ref, query_ref, *refs):
    kv_refs = refs[:count]
    out_ref, scores_ref, value_ref = refs[count:]
    rank = rank_ref[0]
    rows = query_ref.shape[0]
    stacked = jnp.concatenate(
        [query_ref[:, g * HD : (g + 1) * HD] for g in range(GROUP)], axis=0
    )
    maxima = None
    for k in range(count):
        part = dot(stacked, kv_refs[k][:, :HD], NT) * (1.0 / math.sqrt(HD))
        if k == 0:
            row = lax.broadcasted_iota(jnp.int32, part.shape, 0) % rows
            col = lax.broadcasted_iota(jnp.int32, part.shape, 1)
            part = jnp.where(row >= col, part, -1e30)
        else:
            earlier = jnp.bitwise_xor(rank, k) < rank
            part = jnp.where(earlier, part, -1e30)
        scores_ref[:, k * rows : (k + 1) * rows] = part
        value_ref[k * rows : (k + 1) * rows, :] = kv_refs[k][:, HD:]
        peak = jnp.max(part, axis=1, keepdims=True)
        maxima = peak if maxima is None else jnp.maximum(maxima, peak)
    terms = jnp.exp(scores_ref[...] - maxima)
    total = jnp.sum(terms, axis=1, keepdims=True)
    result = dot(terms.astype(BF16), value_ref[...]) / total
    result = result.astype(BF16)
    for g in range(GROUP):
        out_ref[:, g * HD : (g + 1) * HD] = result[g * rows : (g + 1) * rows, :]


def partner_sums(blocks, count):
    arrived = [swap(blocks[k + 1], "seq", count, 1) for k in range(0, count, 2)]
    return [
        (blocks[k].astype(F32) + arrived[k // 2].astype(F32)).astype(BF16)
        for k in range(0, count, 2)
    ]


def owner_pieces(sums, count):
    return [sums[0]] + [swap(sums[k // 2], "seq", count, k) for k in range(2, count, 2)]


class Copies:
    def __init__(self, semaphores):
        self.semaphores = semaphores
        self.count = 0

    def start(self, source, target):
        copy = pltpu.make_async_copy(source, target, self.semaphores.at[self.count])
        self.count += 1
        copy.start()
        return copy


def own_kernel(count, rank_ref, *refs):
    own_refs = refs[:count]
    weight_ref, residual_ref, acc_ref, left_ref = refs[count:]
    rank = rank_ref[0]
    rows = own_refs[0].shape[0]
    for k in range(count):
        left_ref[k * rows : (k + 1) * rows, :] = own_refs[k][...]
    tile = 2 * rows
    for t in range(count // 2):
        total = dot(left_ref[t * tile : (t + 1) * tile, :], weight_ref[...])
        for half in range(2):
            k = 2 * t + half
            first = pl.multiple_of(jnp.bitwise_xor(rank, k) * rows, rows)
            rest = residual_ref[pl.ds(first, rows), :].astype(F32)
            acc_ref[k * rows : (k + 1) * rows, :] = (
                total[half * rows : (half + 1) * rows] + rest
            ).astype(BF16)


def mix_kernel(count, used, rank_ref, *refs):
    far_refs = refs[:count]
    weight_refs = refs[count : count + used]
    refs = refs[count + used :]
    acc_ref, gain_ref, in_ref = refs[:3]
    path_refs, gate_refs = refs[3 : count + 3], refs[count + 3 : 2 * count + 3]
    left, weights, normed, mixed, halos, squares, semaphores = refs[2 * count + 3 :]
    rank = rank_ref[0]
    rows = far_refs[0].shape[0]
    width = weight_refs[0].shape[0]
    channels = in_ref.shape[0] // 2
    copies = Copies(semaphores)
    tile = rows * count // 2
    spans = [pl.ds(r * width, width) for r in range(used)]
    weight_copies = [copies.start(weight_refs[0], weights.at[spans[0], :])]
    left_copies, out_copies = [], []
    for t in range(2):
        left_copies.append(
            [
                copies.start(
                    far_refs[k],
                    left.at[pl.ds(k * rows, rows), :],
                )
                for k in range(t * count // 2, (t + 1) * count // 2)
            ]
        )
        if t == 0:
            for r in range(1, used):
                weight_copies.append(copies.start(weight_refs[r], weights.at[spans[r], :]))
    eye = lax.broadcasted_iota(jnp.int32, (rows, rows), 0) == lax.broadcasted_iota(
        jnp.int32, (rows, rows), 1
    )
    for t in range(2):
        span = pl.ds(t * tile, tile)
        for copy in left_copies[t]:
            copy.wait()
        hidden = acc_ref[span, :].astype(F32)
        for r in range(used):
            if t == 0:
                weight_copies[r].wait()
            hidden += dot(left[span, spans[r]], weights[spans[r], :])
        normed[span, :] = (hidden * gain_ref[...]).astype(BF16)
        sums = jnp.sum(hidden * hidden, axis=1, keepdims=True)
        for part in range(count // 2):
            k = t * count // 2 + part
            squares[k : k + 1, :] = jnp.sum(
                jnp.where(eye, sums[part * rows : (part + 1) * rows], 0.0),
                axis=0,
                keepdims=True,
            )
    for t in range(2):
        result = dot(normed[pl.ds(t * tile, tile), :], in_ref[...], NT).astype(BF16)
        mixed[pl.ds(t * tile, tile), :] = result
        for part in range(count // 2):
            k = t * count // 2 + part
            block = mixed.at[pl.ds(k * rows, rows), :]
            target = path_refs[k].at[pl.ds(HALO, rows), :]
            out_copies.append(copies.start(block.at[:, pl.ds(0, channels)], target))
            out_copies.append(copies.start(block.at[:, pl.ds(channels, channels)], gate_refs[k]))
    line = lax.broadcasted_iota(jnp.int32, (HALO, channels), 0)
    for k in range(count):
        block = jnp.bitwise_xor(rank, k)
        before = jnp.bitwise_xor(rank, jnp.maximum(block - 1, 0))
        last = pl.multiple_of(before * rows + (rows - HALO), HALO)
        halo = mixed[pl.ds(last, HALO), :channels].astype(F32)
        own = jnp.tile(squares[k : k + 1, :], (1, channels // rows))
        past = jnp.tile(squares[pl.ds(before, 1), :], (1, channels // rows))
        halo = jnp.where(line == 0, own, jnp.where(line == 1, past, halo))
        halos[k] = halo.astype(BF16)
        out_copies.append(copies.start(halos.at[k], path_refs[k].at[pl.ds(0, HALO), :]))
    for copy in out_copies:
        copy.wait()


def conv_kernel(n_pieces, count, rank_ref, *refs):
    piece_refs = refs[:n_pieces]
    param_refs = refs[n_pieces : n_pieces + count]
    out_ref, maps_ref, scale_ref, total_ref = refs[n_pieces + count :]
    rank = rank_ref[0]
    total = piece_refs[0][...].astype(F32)
    for piece in piece_refs[1:]:
        total += piece[...].astype(F32)
    rows = total.shape[0] - HALO
    eye = lax.broadcasted_iota(jnp.int32, (rows, rows), 0) == lax.broadcasted_iota(
        jnp.int32, (rows, rows), 1
    )
    scale_own = lax.rsqrt(total[0:1, :rows] / D + NORM_EPS)
    scale_past = lax.rsqrt(total[1:2, :rows] / D + NORM_EPS)
    scale_past = jnp.where(rank == 0, 0.0, scale_past)
    column_own = jnp.sum(jnp.where(eye, scale_own, 0.0), axis=1, keepdims=True)
    column_past = jnp.sum(jnp.where(eye, scale_past, 0.0), axis=1, keepdims=True)
    scale_ref[...] = column_own + jnp.zeros(scale_ref.shape, F32)
    total_ref[0:8, :] = total[HALO - 8 : HALO] * column_past[rows - 8 :]
    total_ref[8:, :] = total[HALO:] * column_own
    param_rows, group = param_refs[0].shape
    middle = DT_RANK + 2 * NST
    lane = lax.broadcasted_iota(jnp.int32, (param_rows, group), 1)
    parity = lane // (group // 2) == rank % 2
    projected = jnp.zeros((middle, rows), F32)
    for m in range(count // 2):
        first = pl.multiple_of(jnp.bitwise_xor(rank, 2 * m) // 2 * group, group)
        path = total_ref[:, pl.ds(first, group)]
        params = jnp.where(
            parity, param_refs[2 * m][...].astype(F32), param_refs[2 * m + 1][...].astype(F32)
        )
        taps = params[middle : middle + 5] + params[middle + 5 : middle + 10]
        taps += params[middle + 10 : middle + 15]
        conv = taps[CONV : CONV + 1] + jnp.zeros((rows, group), F32)
        for offset in range(CONV):
            begin = 8 - (CONV - 1) + offset
            conv += taps[offset : offset + 1] * path[begin : begin + rows]
        result = (conv / (1.0 + jnp.exp(-conv))).astype(BF16)
        out_ref[:, pl.ds(first, group)] = result
        projected += dot(params[0:middle].astype(BF16), result, NT)
    low_rank = projected[:DT_RANK]
    maps = projected[DT_RANK:]
    high = maps.astype(BF16)
    maps_ref[0:DT_RANK, :] = low_rank.astype(BF16)
    maps_ref[DT_RANK:middle, :] = high
    maps_ref[middle:, :] = (maps - high.astype(F32)).astype(BF16)


def sum_kernel(n_maps, n_gates, count, rank_ref, *refs):
    map_refs = refs[:n_maps]
    gate_refs = refs[n_maps : n_maps + n_gates]
    refs = refs[n_maps + n_gates :]
    inputs_ref, scale_ref = refs[:2]
    out_refs = refs[2 : 2 + count // 2]
    gate_scratch = refs[2 + count // 2]
    rank = rank_ref[0]
    total = map_refs[0][...].astype(F32)
    for piece in map_refs[1:]:
        total += piece[...].astype(F32)
    middle = DT_RANK + 2 * NST
    maps = total[DT_RANK:middle] + total[middle:]
    high = maps.astype(BF16)
    low = (maps - high.astype(F32)).astype(BF16)
    low_rank = total[:DT_RANK].astype(BF16)
    gate = gate_refs[0][...].astype(F32)
    for piece in gate_refs[1:]:
        gate += piece[...].astype(F32)
    gate = gate * scale_ref[:, 0:1]
    gate_scratch[...] = gate / (1.0 + jnp.exp(-gate))
    rows, group = scale_ref.shape
    lane = lax.broadcasted_iota(jnp.int32, (rows, group), 1)
    for at, out_ref in enumerate(out_refs):
        first = pl.multiple_of(jnp.bitwise_xor(rank, 2 * at) // 2 * group, group)
        inputs = inputs_ref[:, pl.ds(first, group)].astype(F32)
        gate = gate_scratch[:, pl.ds(first, group)]
        even = jnp.where(lane < group // 2, inputs, pltpu.roll(gate, group // 2, 1))
        odd = jnp.where(lane < group // 2, pltpu.roll(inputs, group // 2, 1), gate)
        out_ref[0:rows, :] = jnp.where(rank % 2 == 0, even, odd).astype(BF16)
        out_ref[rows : 2 * rows, :] = jnp.where(rank % 2 == 0, odd, even).astype(BF16)
        out_ref[2 * rows : 2 * rows + DT_RANK, :] = low_rank
        out_ref[2 * rows + DT_RANK : 2 * rows + middle, :] = high
        out_ref[2 * rows + middle :, :] = low


def scan_kernel(count, rank_ref, *refs):
    rows = (refs[0].shape[0] - DT_RANK - 4 * NST) // 2
    pair_refs = [refs[k].at[pl.ds(k % 2 * rows, rows), :] for k in range(count)]
    maps_refs = [refs[k].at[pl.ds(2 * rows, DT_RANK + 4 * NST), :] for k in range(count)]
    (
        weight_ref, bias_ref, decay_ref, skip_ref, out_ref,
        factor_ref, source_ref, read_ref, value_ref, end_ref, product_ref, begin_ref,
    ) = refs[count:]
    rank = rank_ref[0]
    pitch = rows + PAD
    lanes = weight_ref.shape[1]
    half = lanes // 2
    groups = NST // 2
    wide = groups * lanes
    map_rows = maps_refs[0].shape[0] - DT_RANK
    map_row = lax.broadcasted_iota(jnp.int32, (map_rows, wide), 0) % (2 * NST)
    state_of = lax.broadcasted_iota(jnp.int32, (map_rows, wide), 1) // half
    spread_in = jnp.where(map_row == state_of, 1.0, 0.0).astype(BF16)
    spread_out = jnp.where(map_row == state_of + NST, 1.0, 0.0).astype(BF16)
    lane = lax.broadcasted_iota(jnp.int32, (rows, lanes), 1)
    for k in range(count):
        span = slice(k * rows, (k + 1) * rows)
        padded = slice(k * pitch, k * pitch + rows)
        step = dot(maps_refs[k][:DT_RANK, :], weight_ref[...], TN) + bias_ref[...]
        step = jnp.maximum(step, 0.0) + jnp.log1p(jnp.exp(-jnp.abs(step)))
        pair = pair_refs[k][...].astype(F32)
        value = jnp.where(lane < half, pair, pltpu.roll(pair, half, 1))
        value_ref[span, :] = value
        maps = maps_refs[k][DT_RANK:, :]
        in_map = dot(maps, spread_in, TN)
        read_ref[span, :] = dot(maps, spread_out, TN)
        drive = step * value
        for g in range(groups):
            part = slice(g * lanes, (g + 1) * lanes)
            factor_ref[g, padded, :] = jnp.exp(step * decay_ref[:, part])
            source_ref[g, padded, :] = drive * in_map[:, part]

    def advance(t, carried):
        at = pl.ds(t, count, stride=pitch)
        following = []
        for g in range(groups):
            state, product = carried[g]
            factor = factor_ref[g, at, :]
            state = factor * state + source_ref[g, at, :]
            product = factor * product
            source_ref[g, at, :] = state
            factor_ref[g, at, :] = product
            following.append((state, product))
        return following

    carried = lax.fori_loop(
        0,
        rows,
        advance,
        [(jnp.zeros((count, lanes), F32), jnp.ones((count, lanes), F32))] * groups,
        unroll=8,
    )
    state = jnp.concatenate([pair[0] for pair in carried], axis=1)
    product = jnp.concatenate([pair[1] for pair in carried], axis=1)
    end_ref[...] = state
    product_ref[...] = product
    carried = jnp.zeros((1, wide), F32)
    for j in range(count):
        at = pl.ds(jnp.bitwise_xor(rank, j), 1)
        begin_ref[at, :] = carried
        carried = product_ref[at, :] * carried + end_ref[at, :]
    for k in range(count):
        span = slice(k * rows, (k + 1) * rows)
        padded = slice(k * pitch, k * pitch + rows)
        total = skip_ref[...] * value_ref[span, :]
        readout = jnp.zeros((rows, lanes), F32)
        for g in range(groups):
            part = slice(g * lanes, (g + 1) * lanes)
            state = source_ref[g, padded, :] + factor_ref[g, padded, :] * begin_ref[k : k + 1, part]
            readout += state * read_ref[span, part]
        total += readout + pltpu.roll(readout, half, 1)
        result = jnp.transpose(total * pair_refs[k][...].astype(F32))
        first = pl.multiple_of(jnp.bitwise_xor(rank, k) * rows, rows)
        out_ref[:, pl.ds(first, rows)] = result[half:].astype(BF16)


def scan_arguments(dt_weight, dt_bias, a_log, skip_gain):
    weight = jnp.concatenate([dt_weight, dt_weight], axis=1)
    bias = jnp.concatenate([dt_bias, dt_bias]).reshape(1, -1)
    skip = jnp.concatenate([skip_gain, skip_gain]).reshape(1, -1)
    decay = (-jnp.exp(a_log)).T.reshape(1, -1)
    return weight, bias, decay, skip


def body(
    n_seq,
    n_sec,
    queries,
    keys,
    values,
    residual,
    out_weight,
    norm_gain,
    in_weight,
    conv_weight,
    conv_bias,
    proj_weight,
    dt_weight,
    dt_bias,
    a_log,
    skip_gain,
):
    shape = jax.ShapeDtypeStruct
    rows = queries.shape[0]
    seq_len = residual.shape[0]
    features = residual.shape[1]
    scale = -(-seq_len // 1024)
    own = conv_weight.shape[0]
    channels = n_seq * 2 * own
    rank = lax.axis_index("seq").astype(jnp.int32)
    rank_arg = rank.reshape(1)

    others_at = list(range(1, n_sec))
    far_at = list(range(3, n_sec, 2))
    weights = {r: swap(out_weight, "section", n_sec, r) for r in far_at}
    nearest = swap(out_weight, "section", n_sec, 1)

    pairs, _ = gather_seq([jnp.concatenate([keys, values], axis=1)] * (n_seq // 2), n_seq)
    attended = call(
        functools.partial(attention_kernel, n_seq),
        shape((rows, GROUP * HD), BF16),
        1 + n_seq,
        [pltpu.VMEM((GROUP * rows, seq_len), F32), pltpu.VMEM((seq_len, HD), BF16)],
        flops=4 * GROUP * rows * seq_len * HD,
        size=4 * rows * 4 * HD * n_seq,
        limit=16 * scale,
    )(rank_arg, queries, *pairs)

    far = jnp.concatenate(
        [swap(attended, "section", n_sec, r) for r in others_at], axis=1
    )
    own_pieces, _ = gather_seq([attended] * (n_seq // 2), n_seq)
    far = after(far, nearest)
    for r in range(2, n_sec, 2):
        weights[r] = swap(after(weights[r + 1], far), "section", n_sec, 1)

    width = out_weight.shape[0]
    conv = jnp.concatenate([conv_weight, conv_bias[:, None]], axis=1).T
    terms = [proj_weight.T]
    for _ in range(3):
        high = lax.reduce_precision(conv, 8, 7)
        terms.append(high.astype(BF16))
        conv = conv - high
    params = jnp.concatenate([*terms, jnp.zeros((1, own), BF16)], axis=0)
    params = jnp.concatenate([params, params], axis=1)
    params, _ = gather_seq([after(params, attended)] * (n_seq // 2), n_seq)
    channel_args = scan_arguments(dt_weight, dt_bias, a_log, skip_gain)
    in_columns = jnp.transpose(in_weight, (1, 2, 3, 0)).reshape(channels, features)
    far = after(far, in_columns)

    acc = call(
        functools.partial(own_kernel, n_seq),
        shape((seq_len, features), BF16),
        n_seq + 2,
        [pltpu.VMEM((seq_len, width), BF16)],
        flops=2 * seq_len * features * width,
        size=seq_len * features * 8,
        limit=56,
    )(rank_arg, *own_pieces, out_weight, residual)
    far_pieces, others = gather_seq(
        [far] * (n_seq // 2),
        n_seq,
        acc, nearest, channel_args, *params,
    )
    acc, weights[1], channel_args, *params = others
    used = n_sec - 1
    payloads = call(
        functools.partial(mix_kernel, n_seq, used),
        [shape((HALO + rows, channels // 2), BF16)] * n_seq
        + [shape((rows, channels // 2), BF16)] * n_seq,
        n_seq + used + 3,
        [
            pltpu.VMEM((seq_len, width * used), BF16),
            pltpu.VMEM((used * width, features), BF16),
            pltpu.VMEM((seq_len, features), BF16),
            pltpu.VMEM((seq_len, channels), BF16),
            pltpu.VMEM((n_seq, HALO, channels // 2), BF16),
            pltpu.VMEM((n_seq, rows), F32),
            pltpu.SemaphoreType.DMA((4 * n_seq + used,)),
        ],
        flops=2 * seq_len * features * (width * used + channels),
        size=seq_len * features * 12,
        limit=28 * scale,
        in_place=[pl.ANY] * (n_seq + used) + [pltpu.VMEM] * 3,
        out_place=pl.ANY,
    )(
        rank_arg,
        *far_pieces,
        *[weights[r] for r in others_at],
        acc,
        norm_gain.reshape(1, -1),
        in_columns,
    )

    path_sums = partner_sums(payloads[:n_seq], n_seq)
    path_pieces = owner_pieces(path_sums, n_seq)
    gates = [after(gate, *path_sums) for gate in payloads[n_seq:]]
    gate_pieces = owner_pieces(partner_sums(gates, n_seq), n_seq)

    map_rows = DT_RANK + 4 * NST
    inputs, maps, scales = call(
        functools.partial(conv_kernel, len(path_pieces), n_seq),
        [
            shape((rows, channels // 2), BF16),
            shape((map_rows, rows), BF16),
            shape((rows, 2 * own), F32),
        ],
        len(path_pieces) + n_seq,
        [pltpu.VMEM((rows + 8, channels // 2), F32)],
        flops=rows * channels * map_rows,
        size=rows * channels * 6,
        limit=12 * scale,
    )(rank_arg, *path_pieces, *params)

    map_parts = [maps] + [swap(maps, "section", n_sec, r) for r in range(1, n_sec)]
    messages = call(
        functools.partial(sum_kernel, n_sec, len(gate_pieces), n_seq),
        [shape((2 * rows + map_rows, rows), BF16)] * (n_seq // 2),
        n_sec + len(gate_pieces) + 2,
        [pltpu.VMEM((rows, channels // 2), F32)],
        size=map_rows * rows * 2 * n_sec,
        limit=8 * scale,
    )(rank_arg, *map_parts, *gate_pieces, inputs, scales)
    scan_pieces = []
    for k in range(0, n_seq, 2):
        piece = swap(messages[k // 2], "seq", n_seq, k) if k else messages[0]
        scan_pieces += [piece, swap(piece, "seq", n_seq, 1)]

    wide = NST * own
    return call(
        functools.partial(scan_kernel, n_seq),
        shape((own, seq_len), BF16),
        n_seq + 4,
        [pltpu.VMEM((NST // 2, n_seq * (rows + PAD), 2 * own), F32)] * 2
        + [pltpu.VMEM((seq_len, wide), F32)]
        + [pltpu.VMEM((seq_len, 2 * own), F32)]
        + [pltpu.VMEM((n_seq, wide), F32)] * 3,
        flops=2 * seq_len * DT_RANK * own,
        size=seq_len * wide * 8,
        limit=16 * scale,
    )(rank_arg, *scan_pieces, *channel_args)


def solution(mesh):
    return jax.shard_map(
        functools.partial(body, mesh.shape["seq"], mesh.shape["section"]),
        mesh=mesh,
        in_specs=(
            P("seq", "section"),
            P("seq", "section"),
            P("seq", "section"),
            P(None, "seq"),
            P("section", "seq"),
            P("seq"),
            P("seq", None, None, "section"),
            P(("seq", "section"), None),
            P(("seq", "section")),
            P(("seq", "section"), None),
            P(None, ("seq", "section")),
            P(("seq", "section")),
            P(("seq", "section"), None),
            P(("seq", "section")),
        ),
        out_specs=P(("seq", "section"), None),
        check_vma=False,
    )
```
